256 devices in a mesh: pool: 2 (over x_hi), group: 8 (over y, core), tp: 16 (over z, x_lo).
Axes of the slice: x: 4 (x_hi: 2, x_lo: 2; x = x_hi * 2 + x_lo), y: 4, z: 8, core: 2. Of those that a mesh axis runs over, the one named last changes fastest.
Arguments:
- cache: bfloat16 [2, 8, 64, 128, 16, 256], P('pool', 'group', None, None, 'tp'), may hold values from -6 to 6
- table: int32 [2, 8, 64], P('pool', 'group'), may hold values from 0 to 63, each once within a row
- lengths: int32 [2, 8, 16], P('pool', 'group'), may hold values from 1 to 512, 4096 in all within a row
- query: bfloat16 [2, 8, 16, 4096], P('pool', 'group', None, 'tp'), may hold values from -6 to 6
- step_kv: bfloat16 [2, 8, 16, 16, 256], P('pool', 'group', None, 'tp'), may hold values from -6 to 6
- resid: bfloat16 [2, 8, 16, 5120], P('pool', 'group'), may hold values from -3 to 3
- new_cache: bfloat16 [2, 8, 16, 256, 16, 256], P('pool', 'group', None, None, 'tp'), may hold values from -6 to 6
- new_lengths: int32 [2, 8, 16], P('pool', 'group'), may hold values from 1 to 255, 2048 in all within a row
- new_query: bfloat16 [2, 8, 16, 4096], P('pool', 'group', None, 'tp'), may hold values from -6 to 6
- new_step_kv: bfloat16 [2, 8, 16, 16, 256], P('pool', 'group', None, 'tp'), may hold values from -6 to 6
- new_resid: bfloat16 [2, 8, 16, 5120], P('pool', 'group'), may hold values from -3 to 3
- pairing: int32 [2, 8, 16, 1], P('pool', 'group'), may hold values from 0 to 15; in each aligned block of 16 rows (0 to 15, 16 to 31, ..., all dimensions but the last counted through in order) at most 2 rows name the same one
- o_weight: bfloat16 [4096, 5120], P('tp'), may hold values from -2 to 2
- norm_gain: bfloat16 [5120], replicated, may hold values from 0.099609375 to 1.8984375
Outputs:
- hidden: bfloat16 [2, 8, 48, 5120], P('pool', 'group')
- normed: bfloat16 [2, 8, 48, 5120], P('pool', 'group')
- slot_cache: bfloat16 [2, 8, 32, 256, 16, 256], P('pool', 'group', None, None, 'tp')
The draws below stay inside these ranges and needn't reach their ends.
Inputs may be any that keep to these rules, and one draw needn't show every extreme that they name: `table`: each group's block ids, each once; request r owns entries r * 4 to r * 4 + 3. `lengths`: some request of each group fills all its 4 blocks. `new_lengths`: some request of each group has the longest prompt, leaving one free position. `pairing`: a group index pool * number of groups + group; no group sends more than 2 requests to one destination, and in some groups exactly 2.
All inputs are finite; a program needn't handle non-finite values.
Results may differ from the reference program's by a relative error of at most 0.0059.
Values may be sent and summed in bfloat16 or wider, within the bound.
No kernel may reach another device: no remote copies, remote signals or barrier semaphores. Data moves between devices by JAX's collectives and lax.ppermute only.
A program may use at most 64 MiB of HBM per device.

```python
import math
import jax
import jax.numpy as jnp
import numpy as np
from jax import lax

D = 5120
HD = 128
QH = 32
BLOCK = 128
NB = 4
NBN = 2
REQ = 16
NEW = 16
KVC = 16
NG2 = 16
CAP = 2
SLOTS = 32
BLK = 64
ROWS = 48
N_POOL = 2
N_GROUP = 8


def query_draw(key, lead):
    law_key = jax.random.fold_in(key, 0)
    shape = (N_POOL, N_GROUP, lead, QH, HD)
    base = jax.random.truncated_normal(law_key, -6.0, 6.0, shape, jnp.float32)
    return base.reshape(N_POOL, N_GROUP, lead, QH * HD).astype(jnp.bfloat16)


def kv_draw(key, shape):
    law_key = jax.random.fold_in(key, 0)
    base = jax.random.truncated_normal(law_key, -6.0, 6.0, shape, jnp.float32)
    return base.astype(jnp.bfloat16)


def draw_query(key, part):
    key = jax.random.fold_in(key, 1)
    return query_draw(key, REQ)


def draw_new_query(key, part):
    key = jax.random.fold_in(key, 2)
    return query_draw(key, NEW)


def draw_cache(key, part):
    key = jax.random.fold_in(key, 3)
    return kv_draw(key, (N_POOL, N_GROUP, BLK, BLOCK, KVC, 2 * HD))


def draw_new_cache(key, part):
    key = jax.random.fold_in(key, 4)
    return kv_draw(key, (N_POOL, N_GROUP, NEW, NBN * BLOCK, KVC, 2 * HD))


def draw_step_kv(key, part):
    key = jax.random.fold_in(key, 5)
    return kv_draw(key, (N_POOL, N_GROUP, REQ, KVC, 2 * HD))


def draw_new_step_kv(key, part):
    key = jax.random.fold_in(key, 6)
    return kv_draw(key, (N_POOL, N_GROUP, NEW, KVC, 2 * HD))


def draw_o_weight(key, part):
    key = jax.random.fold_in(key, 7)
    law_key, scale_key = jax.random.split(key)
    column = jnp.arange(D, dtype=jnp.float32) / D
    spread = jnp.exp(math.log(3.0) * column + math.log(10.0) * jax.random.uniform(scale_key, (D,), jnp.float32))
    base = jax.random.truncated_normal(law_key, -4.0, 4.0, (QH * HD, D), jnp.float32)
    return (base * spread[None, :] * (0.3 / math.sqrt(QH * HD))).astype(jnp.bfloat16)


def level_of(key, extent, pieces, low, top_value):
    factor_of = 1.0
    for dim, parts in pieces:
        draws = jax.random.uniform(jax.random.fold_in(jax.random.fold_in(key, 6), dim), (parts,), jnp.float32, low / len(pieces), top_value / len(pieces))
        factor_of = factor_of * jnp.repeat(jnp.exp(draws), extent[dim] // parts).reshape((-1,) + (1,) * (len(extent) - 1 - dim))
    return factor_of


def length_profile(amount, total, reach, lean):
    loads = [(1 << 20) // math.isqrt(rank ** lean) + 1 for rank in range(2, amount + 1)]
    surplus, given = total - reach - (amount - 1), [1] * (amount - 1)
    while surplus > 0:
        candidates = [i for i in range(amount - 1) if given[i] < reach]
        mass, remaining = sum([loads[i] for i in candidates]), surplus
        for i in candidates:
            extra = min(reach - given[i], max(1, remaining * loads[i] // mass), surplus)
            given[i] = given[i] + extra
            surplus = surplus - extra
    return np.array([reach] + given)


def ragged_sizes(stream_key, amount, total, most, skew):
    if amount == 2:
        one = jax.random.randint(stream_key, (), max(1, total - most), min(most, total - 1) + 1)
        return jnp.stack([one, total - one])
    tallies = jnp.asarray(length_profile(amount, total, most, skew), jnp.int32)
    twos = (amount - 1) // 2
    donor, sink = tallies[1:1 + 2 * twos:2], tallies[2:2 + 2 * twos:2]
    slack = jnp.minimum(donor - 1, most - sink)
    passed = jax.random.randint(jax.random.fold_in(stream_key, 1), (twos,), 0, 1 << 20) % (slack + 1)
    tallies = tallies.at[1:1 + 2 * twos:2].set(donor - passed).at[2:2 + 2 * twos:2].set(sink + passed)
    return tallies[jax.random.permutation(jax.random.fold_in(stream_key, 2), amount)]


def assign_block(rng, own, number, rows, number_of, top, reach, slope):
    sequence = jax.random.permutation(rng, number_of)
    packed, common = portions_of(number_of, rows * top, reach, slope, True), portions_of(number_of, rows * top, reach, slope, False)
    places = jnp.arange(number_of)

    def named(sizes, turn):
        used = int((sizes > 0).sum())
        fixed = max(1, used // 4)
        moved = fixed + (places - fixed + turn * (used - fixed)) % max(1, number_of - fixed)
        return jnp.zeros((number_of,), jnp.int32).at[sequence[jnp.where(places < fixed, places, moved)]].set(jnp.asarray(sizes, jnp.int32))

    sizes = jnp.where(number % 4 == 0, named(packed, number // 4), named(common, number - number // 4 - 1))
    mixed = jax.random.permutation(jax.random.fold_in(own, 3), number_of)
    source_of, sink = mixed[0:number_of // 2 * 2:2], mixed[1:number_of // 2 * 2:2]
    margin = jnp.minimum(sizes[source_of] - 1, reach - sizes[sink]) // 2
    margin = jnp.where((source_of == sequence[0]) | (sink == sequence[0]) | (sizes[sink] == 0), 0, jnp.maximum(margin, 0))
    moved = jax.random.randint(jax.random.fold_in(own, 4), (number_of // 2,), 0, 1 << 20) % (margin + 1)
    sizes = sizes.at[source_of].add(-moved).at[sink].add(moved)
    labels = jnp.searchsorted(jnp.cumsum(sizes), jnp.arange(rows * top), side="right").astype(jnp.int32)
    grid = labels.reshape(top, rows).T
    grid = grid[jax.random.permutation(jax.random.fold_in(own, 1), rows)]
    turn = jax.random.randint(jax.random.fold_in(own, 2), (rows, 1), 0, top)
    return jnp.take_along_axis(grid, (jnp.arange(top)[None, :] + turn) % top, axis=1)


def portions_of(count, total, limit, slope, full):
    loads = [(1 << 20) // math.isqrt(rank ** slope) + 1 for rank in range(1, count + 1)]
    largest = limit if full else min(limit, max(-(-total // count), total * loads[0] // sum(loads)))
    least = 1 if total - largest >= count - 1 else 0
    counts, spare = [largest] + [least] * (count - 1), total - largest - least * (count - 1)
    while spare > 0:
        free = [i for i in range(1, count) if counts[i] < largest] or [i for i in range(1, count) if counts[i] < limit]
        whole, remaining = sum([loads[i] for i in free]), spare
        for i in free:
            addition = min(limit - counts[i], max(1, remaining * loads[i] // whole), spare)
            counts[i] = counts[i] + addition
            spare = spare - addition
    return np.array(counts)


def bell_draw(key, shape, scale, limit, shards=(), kind=jnp.bfloat16):
    factor_of = level_of(key, shape, shards, -0.22, 0.18) if shards else 1.0
    entries = jax.random.normal(key, shape, jnp.float32) * scale * factor_of
    return jnp.minimum(jnp.maximum(entries, -limit), limit).astype(kind)


def setup_inputs(seed: int = 0) -> dict:
    arg_keys = jax.random.split(jax.random.key(seed), 15)
    cache = draw_cache(jax.random.fold_in(arg_keys[14], 71), 0)
    table = jax.vmap(lambda own: jax.random.permutation(own, BLK))(jax.random.split(arg_keys[1], N_POOL * N_GROUP)).reshape((N_POOL, N_GROUP, BLK)).astype(jnp.int32)
    lengths = jax.vmap(lambda own: ragged_sizes(own, REQ, REQ * NB * BLOCK // 2, NB * BLOCK, 2))(jax.random.split(arg_keys[2], N_POOL * N_GROUP)).reshape((N_POOL, N_GROUP, REQ)).astype(jnp.int32)
    query = draw_query(jax.random.fold_in(arg_keys[14], 71), 0)
    step_kv = draw_step_kv(jax.random.fold_in(arg_keys[14], 71), 0)
    resid = bell_draw(arg_keys[5], (N_POOL, N_GROUP, REQ, D), 0.5, 3.0, ((0, 2), (1, 8)))
    new_cache = draw_new_cache(jax.random.fold_in(arg_keys[14], 71), 0)
    new_lengths = jax.vmap(lambda own: ragged_sizes(own, NEW, NEW * NBN * BLOCK // 2, NBN * BLOCK - 1, 2))(jax.random.split(arg_keys[7], N_POOL * N_GROUP)).reshape((N_POOL, N_GROUP, NEW)).astype(jnp.int32)
    new_query = draw_new_query(jax.random.fold_in(arg_keys[14], 71), 0)
    new_step_kv = draw_new_step_kv(jax.random.fold_in(arg_keys[14], 71), 0)
    new_resid = bell_draw(arg_keys[10], (N_POOL, N_GROUP, NEW, D), 0.5, 3.0, ((0, 2), (1, 8)))
    pairing_keys = jax.random.split(jax.random.fold_in(arg_keys[11], 1), N_POOL * N_GROUP * NEW // NEW)
    pairing_turns = jax.random.permutation(jax.random.fold_in(arg_keys[11], 3), N_POOL * N_GROUP * NEW // NEW)
    pairing = jax.vmap(lambda own, number: assign_block(jax.random.fold_in(arg_keys[11], 2), own, number, NEW, NG2, 1, CAP, 2))(pairing_keys, pairing_turns).reshape((N_POOL, N_GROUP, NEW, 1))
    o_weight = draw_o_weight(jax.random.fold_in(arg_keys[14], 71), 0)
    norm_gain = jnp.clip(1.0 + 0.18 * jax.random.normal(arg_keys[13], (D,), jnp.float32), 0.099609375, 1.8984375).astype(jnp.bfloat16)
    return dict(cache=cache, table=table, lengths=lengths, query=query, step_kv=step_kv, resid=resid, new_cache=new_cache, new_lengths=new_lengths, new_query=new_query, new_step_kv=new_step_kv, new_resid=new_resid, pairing=pairing, o_weight=o_weight, norm_gain=norm_gain)


def attend(query_rows, kv_rows, own_kv, length):
    row_count, tokens, kv_heads, pair_width = kv_rows.shape
    head_dim = pair_width // 2
    grouped = query_rows.astype(jnp.float32).reshape(row_count, kv_heads, -1, head_dim)
    key_part = kv_rows[..., :head_dim].astype(jnp.float32)
    value_part = kv_rows[..., head_dim:].astype(jnp.float32)
    own_key = own_kv[..., :head_dim].astype(jnp.float32)
    own_value = own_kv[..., head_dim:].astype(jnp.float32)
    scaling = 1.0 / math.sqrt(head_dim)
    scores = jnp.einsum('rcgd,rtcd->rcgt', grouped, key_part) * scaling
    own_score = jnp.einsum('rcgd,rcd->rcg', grouped, own_key) * scaling
    position = jnp.arange(tokens, dtype=jnp.int32)
    visible = (position[None, :] < length[:, None])[:, None, None, :]
    highest = jnp.maximum(lax.optimization_barrier(jnp.max(jnp.where(visible, scores, -1e+30), axis=-1)), own_score)
    exponent = jnp.where(visible, jnp.exp(scores - highest[..., None]), 0.0)
    own_exponent = jnp.exp(own_score - highest)
    denominator = lax.optimization_barrier(jnp.sum(exponent, axis=-1)) + own_exponent
    weights = (exponent / denominator[..., None]).astype(jnp.bfloat16)
    own_weight = (own_exponent / denominator).astype(jnp.bfloat16)
    blended = jnp.einsum('rcgt,rtcd->rcgd', weights.astype(jnp.float32), value_part)
    blended = blended + own_weight.astype(jnp.float32)[..., None] * own_value[:, :, None, :]
    return blended.astype(jnp.bfloat16).reshape(row_count, -1)

def append_token(kv_rows, own_kv, length):
    position = jnp.arange(kv_rows.shape[1], dtype=jnp.int32)
    place_here = (position[None, :] == length[:, None])[:, :, None, None]
    return jnp.where(place_here, own_kv[:, None], kv_rows)

def slot_targets(pairing):
    target_group = pairing.reshape(NG2, NEW).astype(jnp.int32)
    position = jnp.arange(NEW, dtype=jnp.int32)
    matches = (target_group[:, :, None] == target_group[:, None, :]) & (position[None, None, :] < position[None, :, None])
    rank_within = lax.optimization_barrier(jnp.sum(matches.astype(jnp.int32), axis=-1)).astype(jnp.int32)
    source = jnp.arange(NG2, dtype=jnp.int32)[:, None]
    return (target_group * SLOTS + source * CAP + rank_within).reshape(-1)

def finish(resid_rows, attended_rows, o_weight, norm_gain):
    projected = jnp.dot(attended_rows, o_weight, preferred_element_type=jnp.float32)
    hidden = (resid_rows.astype(jnp.float32) + projected).astype(jnp.bfloat16)
    widened = lax.optimization_barrier(hidden).astype(jnp.float32)
    inverse = lax.rsqrt(lax.optimization_barrier(jnp.mean(widened * widened, axis=-1, keepdims=True)) + 1e-06)
    normed = (widened * inverse * norm_gain.astype(jnp.float32)).astype(jnp.bfloat16)
    return (hidden, normed)

def reference(cache, table, lengths, query, step_kv, resid, new_cache, new_lengths, new_query, new_step_kv, new_resid, pairing, o_weight, norm_gain):

    def merge_lead(array):
        return array.reshape((NG2,) + array.shape[2:])

    def resident_group(operands):
        cache_group, table_group, length_group, query_group, own_group = operands
        gathered = cache_group[table_group].reshape(REQ, NB * BLOCK, KVC, 2 * HD)
        return attend(query_group, gathered, own_group, length_group)
    resident = lax.map(resident_group, (merge_lead(cache), merge_lead(table), merge_lead(lengths), merge_lead(query), merge_lead(step_kv)))
    target = slot_targets(pairing)

    def deliver(payload):
        flat_rows = payload.reshape((NG2 * NEW,) + payload.shape[3:])
        blank_slots = jnp.zeros((NG2 * SLOTS,) + flat_rows.shape[1:], flat_rows.dtype)
        return blank_slots.at[target].set(flat_rows).reshape((NG2, SLOTS) + flat_rows.shape[1:])

    def slot_group(operands):
        kv_group, query_group, own_group, length_group = operands
        attended = attend(query_group, kv_group, own_group, length_group)
        appended = append_token(kv_group, own_group, length_group)
        return (attended, appended)
    slot_rows, slot_cache = lax.map(slot_group, (deliver(new_cache), deliver(new_query), deliver(new_step_kv), deliver(new_lengths)))
    attended_all = jnp.concatenate([resident, slot_rows], axis=1).reshape(NG2 * ROWS, QH * HD)
    resid_all = jnp.concatenate([merge_lead(resid), deliver(new_resid)], axis=1).reshape(NG2 * ROWS, D)
    hidden, normed = finish(resid_all, attended_all, o_weight, norm_gain)
    return (hidden.reshape(N_POOL, N_GROUP, ROWS, D), normed.reshape(N_POOL, N_GROUP, ROWS, D), slot_cache.reshape(N_POOL, N_GROUP, SLOTS, NBN * BLOCK, KVC, 2 * HD))
```

```python
import functools
import math

import jax
import jax.numpy as jnp
from jax import lax
from jax.experimental import pallas as pl
from jax.experimental.pallas import tpu as pltpu
from jax.sharding import PartitionSpec as P

REQ = 16
HD = 128
NZ = 8
SMEM = pltpu.SMEM
VMEM = pltpu.VMEM
VMEM_LIMIT = 48 * 1024 * 1024


def softmax_parts(scores, own_score, lengths):
    position = lax.broadcasted_iota(jnp.int32, scores.shape, 1)
    visible = position < lengths
    top = jnp.max(jnp.where(visible, scores, -1e30), axis=-1, keepdims=True)
    top = jnp.maximum(top, own_score)
    exponent = jnp.where(visible, jnp.exp(scores - top), 0.0)
    own_exponent = jnp.exp(own_score - top)
    denominator = jnp.sum(exponent, axis=-1, keepdims=True) + own_exponent
    weights = (exponent / denominator).astype(jnp.bfloat16).astype(jnp.float32)
    own_weight = (own_exponent / denominator).astype(jnp.bfloat16).astype(jnp.float32)
    return weights, own_weight


def heads_as_rows(wide):
    return jnp.concatenate([wide[:, :HD], wide[:, HD:]], axis=0)


def attend(query, own, kv_of, ready, length_of, tokens):
    rows = 2 * REQ
    scale = 1.0 / math.sqrt(HD)
    heads = heads_as_rows(query)
    own_key = own[:, :HD].astype(jnp.float32)
    own_value = own[:, HD:].astype(jnp.float32)
    own_key = jnp.concatenate([own_key, own_key], axis=0)
    own_value = jnp.concatenate([own_value, own_value], axis=0)
    own_score = jnp.sum(heads.astype(jnp.float32) * own_key, axis=-1, keepdims=True) * scale
    request = lax.broadcasted_iota(jnp.int32, (rows, 1), 0) % REQ
    lengths = jnp.zeros((rows, 1), jnp.int32)
    scores = jnp.zeros((rows, tokens), jnp.float32)
    for r in range(REQ):
        ready(r)
        lengths = jnp.where(request == r, length_of(r), lengths)
        one = lax.dot_general(
            heads, kv_of(r)[:, :HD], (((1,), (1,)), ((), ())), preferred_element_type=jnp.float32
        )
        scores = jnp.where(request == r, one, scores)
    weights, own_weight = softmax_parts(scores * scale, own_score, lengths)
    total = own_weight * own_value
    for r in range(REQ):
        mine = jnp.where(request == r, weights, 0.0).astype(jnp.bfloat16)
        total = total + jnp.dot(mine, kv_of(r)[:, HD:], preferred_element_type=jnp.float32)
    attended = total.astype(jnp.bfloat16)
    return jnp.concatenate([attended[:REQ], attended[REQ:]], axis=1)


def front_kernel(
    place,
    pairing,
    new_lengths,
    lengths,
    table,
    query,
    own,
    new_query,
    new_own,
    resid,
    new_resid,
    new_cache,
    cache,
    weight,
    send,
    first,
    *rest,
):
    others = rest[: NZ - 1]
    new_buf, kv_buf, w_buf, taken, count, new_sem, kv_sem, w_sem, send_sem = rest[NZ - 1 :]
    z, x_lo = place[0], place[1]
    width = w_buf.shape[1] // NZ

    new_copies = [
        pltpu.make_async_copy(new_cache.at[i], new_buf.at[i], new_sem.at[i]) for i in range(REQ)
    ]
    for copy in new_copies:
        copy.start()
    kv_copies = [
        pltpu.make_async_copy(
            cache.at[table[e]], kv_buf.at[e // 4, pl.ds(e % 4 * 128, 128)], kv_sem.at[e]
        )
        for e in range(4 * REQ)
    ]
    for copy in kv_copies:
        copy.start()
    w_copy = pltpu.make_async_copy(weight, w_buf, w_sem)
    w_copy.start()

    new_buf[REQ] = jnp.zeros(new_buf.shape[1:], new_buf.dtype)
    for j in range(2 * REQ):
        taken[j] = REQ
    for j in range(REQ):
        count[j] = 0
    for i in range(REQ):
        target = pairing[i]
        k = count[target]
        count[target] = k + 1
        taken[2 * target + k] = i

    for i in range(REQ):
        new_copies[i].wait()
        base = pl.multiple_of(new_lengths[i] // 16 * 16, 16)
        window = new_buf[i, pl.ds(base, 16), :].astype(jnp.float32)
        row = lax.broadcasted_iota(jnp.int32, (16, 1), 0)
        token = new_own[i : i + 1, :].astype(jnp.float32)
        window = jnp.where(row == new_lengths[i] - base, token, window)
        new_buf[i, pl.ds(base, 16), :] = window.astype(new_buf.dtype)
    send_copies = [
        pltpu.make_async_copy(new_buf.at[taken[j]], send.at[j], send_sem.at[j])
        for j in range(2 * REQ)
    ]
    for copy in send_copies:
        copy.start()

    new_rows = attend(
        new_query[...],
        new_own[...],
        lambda r: new_buf.at[r],
        lambda r: None,
        lambda r: new_lengths[r],
        new_buf.shape[1],
    )

    def kv_ready(r):
        for b in range(4):
            kv_copies[4 * r + b].wait()

    rows = attend(
        query[...],
        own[...],
        lambda r: kv_buf.at[r],
        kv_ready,
        lambda r: lengths[r],
        kv_buf.shape[1],
    )
    attended = jnp.concatenate([rows, new_rows], axis=0)
    w_copy.wait()
    for k in range(NZ):
        columns = pl.ds(pl.multiple_of((z ^ k) * width, 128), width)
        part = jnp.dot(attended, w_buf[:, columns], preferred_element_type=jnp.float32)
        if k:
            others[k - 1][...] = part.astype(jnp.bfloat16)
        else:
            block = jnp.concatenate([resid[:, columns], new_resid[:, columns]], axis=0)
            first[...] = part + jnp.where(x_lo == 0, block.astype(jnp.float32), 0.0)
    for copy in send_copies:
        copy.wait()


def front(place, pairing, new_lengths, lengths, table, query, own, new_query, new_own, resid, new_resid, new_cache, cache, weight):
    tokens = new_cache.shape[1]
    width = weight.shape[1] // NZ
    any_space = pl.BlockSpec(memory_space=pl.ANY)
    smem = pl.BlockSpec(memory_space=SMEM)
    vmem = pl.BlockSpec(memory_space=VMEM)
    return pl.pallas_call(
        front_kernel,
        out_shape=[
            jax.ShapeDtypeStruct((2 * REQ, tokens, 2 * HD), jnp.bfloat16),
            jax.ShapeDtypeStruct((2 * REQ, width), jnp.float32),
        ]
        + [jax.ShapeDtypeStruct((2 * REQ, width), jnp.bfloat16)] * (NZ - 1),
        in_specs=[smem] * 5 + [vmem] * 6 + [any_space] * 3,
        out_specs=[any_space] + [vmem] * NZ,
        scratch_shapes=[
            VMEM((REQ + 1, tokens, 2 * HD), jnp.bfloat16),
            VMEM((REQ, 4 * cache.shape[1], 2 * HD), jnp.bfloat16),
            VMEM(weight.shape, jnp.bfloat16),
            SMEM((2 * REQ,), jnp.int32),
            SMEM((REQ,), jnp.int32),
            pltpu.SemaphoreType.DMA((REQ,)),
            pltpu.SemaphoreType.DMA((4 * REQ,)),
            pltpu.SemaphoreType.DMA,
            pltpu.SemaphoreType.DMA((2 * REQ,)),
        ],
        compiler_params=pltpu.CompilerParams(vmem_limit_bytes=VMEM_LIMIT),
        cost_estimate=pl.CostEstimate(flops=400_000_000, bytes_accessed=14_000_000, transcendentals=30_000),
        name="front",
    )(place, pairing, new_lengths, lengths, table, query, own, new_query, new_own, resid, new_resid, new_cache, cache, weight)


def add_kernel(first, *refs):
    total = first[...]
    for part in refs[:-1]:
        total = total + part[...].astype(jnp.float32)
    refs[-1][...] = total.astype(jnp.bfloat16)


def route_kernel(place, pairing, left, right, resident, *refs):
    outs, count = refs[:4], refs[4]
    me = place[2]
    hidden = (left[...].astype(jnp.float32) + right[...].astype(jnp.float32)).astype(jnp.bfloat16)
    resident[...] = hidden[:REQ]
    for j in range(REQ):
        count[j] = 0
    row = lax.broadcasted_iota(jnp.int32, (2 * REQ, REQ), 0)
    column = lax.broadcasted_iota(jnp.int32, (2 * REQ, REQ), 1)
    target_row = jnp.zeros((2 * REQ, REQ), jnp.int32)
    for i in range(REQ):
        target = pairing[i]
        k = count[target]
        count[target] = k + 1
        offset = me ^ target
        at = ((offset >> 3) * 2 + (offset & 1)) * 8 + ((offset >> 1) & 3) * 2 + k
        target_row = jnp.where(column == i, at, target_row)
    chosen = jnp.where(row == target_row, 1.0, 0.0).astype(jnp.bfloat16)
    placed = jnp.dot(chosen, hidden[REQ:], preferred_element_type=jnp.float32)
    for g in range(4):
        outs[g][...] = placed[8 * g : 8 * g + 8].astype(jnp.bfloat16)


def finish_kernel(place, gain, *refs):
    blocks, (hidden, normed) = refs[:NZ], refs[NZ:]
    z, me = place[0], place[2]
    rows, width = blocks[0].shape
    slots = rows - REQ
    slot = lax.broadcasted_iota(jnp.int32, (slots, slots), 0)
    column = lax.broadcasted_iota(jnp.int32, (slots, slots), 1)
    offset = (slot >> 1) ^ me
    at = ((offset >> 1) & 3) * 8 + ((offset >> 3) * 2 + (offset & 1)) * 2 + (slot & 1)
    order = jnp.where(column == at, 1.0, 0.0).astype(jnp.bfloat16)
    square = jnp.zeros((rows, 1), jnp.float32)
    for k in range(NZ):
        columns = pl.ds(pl.multiple_of((z ^ k) * width, 128), width)
        block = blocks[k][...]
        placed = jnp.dot(order, block[REQ:], preferred_element_type=jnp.float32)
        wide = jnp.concatenate([block[:REQ].astype(jnp.float32), placed], axis=0)
        hidden[:, columns] = wide.astype(jnp.bfloat16)
        square = square + jnp.sum(wide * wide, axis=-1, keepdims=True)
    inverse = lax.rsqrt(square / (width * NZ) + 1e-06)
    for k in range(NZ):
        columns = slice(k * width, (k + 1) * width)
        wide = hidden[:, columns].astype(jnp.float32)
        normed[:, columns] = (wide * inverse * gain[:, columns].astype(jnp.float32)).astype(
            jnp.bfloat16
        )


def body(
    cache,
    table,
    lengths,
    query,
    step_kv,
    resid,
    new_cache,
    new_lengths,
    new_query,
    new_step_kv,
    new_resid,
    pairing,
    o_weight,
    norm_gain,
):
    pool, group, tp = lax.axis_index("pool"), lax.axis_index("group"), lax.axis_index("tp")
    groups = lax.axis_size("pool") * lax.axis_size("group")
    ranks = lax.axis_size("tp")
    place = jnp.stack([tp // 2, tp % 2, pool * lax.axis_size("group") + group]).astype(jnp.int32)
    pair = pairing[0, 0, :, 0]
    smem = pl.BlockSpec(memory_space=SMEM)
    vmem = pl.BlockSpec(memory_space=VMEM)

    send, first, *others = front(
        place,
        pair,
        new_lengths[0, 0],
        lengths[0, 0],
        table[0, 0],
        query[0, 0],
        step_kv[0, 0, :, 0],
        new_query[0, 0],
        new_step_kv[0, 0, :, 0],
        resid[0, 0],
        new_resid[0, 0],
        new_cache[0, 0, :, :, 0],
        cache[0, 0, :, :, 0],
        o_weight,
    )
    both = ("pool", "group")
    slot_cache = lax.all_to_all(
        send.reshape((groups, 2) + send.shape[1:]), both, split_axis=0, concat_axis=0, tiled=True
    )
    slot_cache = slot_cache.reshape(send.shape)[None, None, :, :, None, :]

    def over_tp(array, flip):
        return lax.ppermute(array, "tp", [(t, t ^ flip) for t in range(ranks)])

    def over_groups(array, flip):
        return lax.ppermute(array, both, [(s, s ^ flip) for s in range(groups)])

    parts = [over_tp(others[k - 1], 2 * k) for k in range(1, NZ)]
    width = first.shape[1]
    half = pl.pallas_call(
        add_kernel,
        out_shape=jax.ShapeDtypeStruct(first.shape, jnp.bfloat16),
        in_specs=[vmem] * NZ,
        out_specs=vmem,
        name="add",
    )(first, *parts)
    other_half = over_tp(half, 1)
    resident, *toward = pl.pallas_call(
        route_kernel,
        out_shape=[jax.ShapeDtypeStruct((REQ, width), jnp.bfloat16)]
        + [jax.ShapeDtypeStruct((8, width), jnp.bfloat16)] * 4,
        in_specs=[smem] * 2 + [vmem] * 2,
        out_specs=[vmem] * 5,
        scratch_shapes=[SMEM((REQ,), jnp.int32)],
        name="route",
    )(place, pair, half, other_half)
    crossed = [toward[0]] + [
        over_groups(toward[g], (g >> 1) * 8 + (g & 1)) for g in range(1, 4)
    ]
    crossed = jnp.stack(crossed).reshape(4, 4, 2, width)
    turned = crossed.transpose(1, 0, 2, 3).reshape(4, 8, width)
    slots = [turned[0]] + [over_groups(turned[y], 2 * y) for y in range(1, 4)]
    block = jnp.concatenate([resident] + slots, axis=0)
    blocks = [block] + [over_tp(block, 2 * k) for k in range(1, NZ)]
    hidden, normed = pl.pallas_call(
        finish_kernel,
        out_shape=[jax.ShapeDtypeStruct((block.shape[0], width * NZ), jnp.bfloat16)] * 2,
        in_specs=[smem] + [vmem] * (NZ + 1),
        out_specs=[vmem] * 2,
        name="finish",
    )(place, norm_gain.reshape(1, -1), *blocks)
    return (hidden[None, None], normed[None, None], slot_cache)


def solution(mesh):
    placed = (
        P("pool", "group", None, None, "tp", None),
        P("pool", "group", None),
        P("pool", "group", None),
        P("pool", "group", None, "tp"),
        P("pool", "group", None, "tp", None),
        P("pool", "group", None, None),
        P("pool", "group", None, None, "tp", None),
        P("pool", "group", None),
        P("pool", "group", None, "tp"),
        P("pool", "group", None, "tp", None),
        P("pool", "group", None, None),
        P("pool", "group", None, None),
        P("tp", None),
        P(),
    )
    return jax.shard_map(
        body,
        mesh=mesh,
        in_specs=placed,
        out_specs=(
            P("pool", "group", None, None),
            P("pool", "group", None, None),
            P("pool", "group", None, None, "tp", None),
        ),
        check_vma=False,
    )
```

```python
import functools
import math

import jax
import jax.numpy as jnp
from jax import lax
from jax.experimental import pallas as pl
from jax.experimental.pallas import tpu as pltpu
from jax.sharding import PartitionSpec as P

REQ = 16
HD = 128
NZ = 8
CUT = 176
SMEM = pltpu.SMEM
VMEM = pltpu.VMEM
VMEM_LIMIT = 63 * 1024 * 1024
SMALL_LIMIT = 8 * 1024 * 1024


def softmax_parts(scores, own_score, lengths):
    position = lax.broadcasted_iota(jnp.int32, scores.shape, 1)
    visible = position < lengths
    top = jnp.max(jnp.where(visible, scores, -1e30), axis=-1, keepdims=True)
    top = jnp.maximum(top, own_score)
    exponent = jnp.where(visible, jnp.exp(scores - top), 0.0)
    own_exponent = jnp.exp(own_score - top)
    denominator = jnp.sum(exponent, axis=-1, keepdims=True) + own_exponent
    weights = (exponent / denominator).astype(jnp.bfloat16).astype(jnp.float32)
    own_weight = (own_exponent / denominator).astype(jnp.bfloat16).astype(jnp.float32)
    return weights, own_weight


def heads_as_rows(wide):
    return jnp.concatenate([wide[:, :HD], wide[:, HD:]], axis=0)


def attend(query, own, kv_of, length_of, tokens):
    rows = 2 * REQ
    scale = 1.0 / math.sqrt(HD)
    heads = heads_as_rows(query)
    own_key = own[:, :HD].astype(jnp.float32)
    own_value = own[:, HD:].astype(jnp.float32)
    own_key = jnp.concatenate([own_key, own_key], axis=0)
    own_value = jnp.concatenate([own_value, own_value], axis=0)
    own_score = jnp.sum(heads.astype(jnp.float32) * own_key, axis=-1, keepdims=True) * scale
    request = lax.broadcasted_iota(jnp.int32, (rows, 1), 0) % REQ
    lengths = jnp.zeros((rows, 1), jnp.int32)
    scores = jnp.zeros((rows, tokens), jnp.float32)
    for r in range(REQ):
        lengths = jnp.where(request == r, length_of(r), lengths)
        one = lax.dot_general(
            heads, kv_of(r)[:, :HD], (((1,), (1,)), ((), ())), preferred_element_type=jnp.float32
        )
        scores = jnp.where(request == r, one, scores)
    weights, own_weight = softmax_parts(scores * scale, own_score, lengths)
    total = own_weight * own_value
    for r in range(REQ):
        mine = jnp.where(request == r, weights, 0.0).astype(jnp.bfloat16)
        total = total + jnp.dot(mine, kv_of(r)[:, HD:], preferred_element_type=jnp.float32)
    attended = total.astype(jnp.bfloat16)
    return jnp.concatenate([attended[:REQ], attended[REQ:]], axis=1)


def group_index():
    return lax.axis_index("pool") * lax.axis_size("group") + lax.axis_index("group")


def pack_kernel(pairing_in, lengths_in, own_in, new_cache, early, late, buf, own, pairing, lengths, taken, count, small_sem, in_sem, early_sem, late_sem):
    small = [
        pltpu.make_async_copy(pairing_in, pairing, small_sem.at[0]),
        pltpu.make_async_copy(lengths_in, lengths, small_sem.at[1]),
        pltpu.make_async_copy(own_in, own, small_sem.at[2]),
    ]
    for copy in small:
        copy.start()
    load = pltpu.make_async_copy(new_cache, buf.at[pl.ds(0, REQ)], in_sem)
    load.start()
    buf[REQ] = jnp.zeros(buf.shape[1:], buf.dtype)
    for j in range(2 * REQ):
        taken[j] = REQ
    for j in range(REQ):
        count[j] = 0
    for copy in small:
        copy.wait()
    for i in range(REQ):
        target = pairing[i]
        k = count[target]
        count[target] = k + 1
        taken[2 * target + k] = i
    row = lax.broadcasted_iota(jnp.int32, (16, 1), 0)
    load.wait()
    for i in range(REQ):
        base = pl.multiple_of(lengths[i] // 16 * 16, 16)
        window = buf[i, pl.ds(base, 16), :].astype(jnp.float32)
        token = own[i : i + 1, :].astype(jnp.float32)
        window = jnp.where(row == lengths[i] - base, token, window)
        buf[i, pl.ds(base, 16), :] = window.astype(buf.dtype)
    cut = early.shape[1]
    for j in range(2 * REQ):
        request = buf.at[taken[j]]
        pltpu.make_async_copy(request.at[pl.ds(0, cut)], early.at[j], early_sem).start()
    for j in range(2 * REQ):
        request = buf.at[taken[j]]
        pltpu.make_async_copy(request.at[pl.ds(cut, late.shape[1])], late.at[j], late_sem).start()
    pltpu.make_async_copy(early, early, early_sem).wait()
    pltpu.make_async_copy(late, late, late_sem).wait()


def pack(pairing, new_lengths, new_own, new_cache):
    tokens = new_cache.shape[1]
    any_space = pl.BlockSpec(memory_space=pltpu.HBM)
    return pl.pallas_call(
        pack_kernel,
        out_shape=[
            jax.ShapeDtypeStruct((2 * REQ, CUT, 2 * HD), jnp.bfloat16),
            jax.ShapeDtypeStruct((2 * REQ, tokens - CUT, 2 * HD), jnp.bfloat16),
        ],
        in_specs=[any_space] * 4,
        out_specs=[any_space] * 2,
        scratch_shapes=[
            VMEM((REQ + 1, tokens, 2 * HD), jnp.bfloat16),
            VMEM(new_own.shape, jnp.bfloat16),
            SMEM((REQ,), jnp.int32),
            SMEM((REQ,), jnp.int32),
            SMEM((2 * REQ,), jnp.int32),
            SMEM((REQ,), jnp.int32),
            pltpu.SemaphoreType.DMA((3,)),
            pltpu.SemaphoreType.DMA,
            pltpu.SemaphoreType.DMA,
            pltpu.SemaphoreType.DMA,
        ],
        compiler_params=pltpu.CompilerParams(vmem_limit_bytes=VMEM_LIMIT),
        cost_estimate=pl.CostEstimate(flops=1_000_000, bytes_accessed=6_400_000, transcendentals=0),
        name="pack",
    )(pairing, new_lengths, new_own, new_cache)


def front_kernel(*refs):
    ins, refs = refs[:13], refs[13:]
    first, one_up, one_down, two_up, two_down, opposite, chosen = refs[:7]
    refs = refs[7:]
    bufs, (count, table_sem, small_sem, new_sem, kv_sem, weight_sem) = refs[:13], refs[13:]
    pairing, lengths, table, new_lengths, query, own, new_query, new_own, resid, new_resid, weight, new_buf, kv_buf = bufs
    new_cache, cache = ins[11], ins[12]
    z, x_lo = lax.axis_index("tp") // 2, lax.axis_index("tp") % 2
    width = weight.shape[1] // NZ

    table_copy = pltpu.make_async_copy(ins[2], table, table_sem)
    table_copy.start()
    small = [pltpu.make_async_copy(ins[n], bufs[n], small_sem.at[n]) for n in range(10) if n != 2]
    new_copy = pltpu.make_async_copy(new_cache, new_buf, new_sem)
    weight_copy = pltpu.make_async_copy(ins[10], weight, weight_sem)
    for copy in small:
        copy.start()
    new_copy.start()
    table_copy.wait()
    for e in range(4 * REQ):
        pltpu.make_async_copy(cache.at[table[e]], kv_buf.at[e], kv_sem).start()
    weight_copy.start()
    for copy in small:
        copy.wait()
    new_copy.wait()

    new_rows = attend(
        new_query[...],
        new_own[...],
        lambda r: new_buf[r],
        lambda r: new_lengths[r],
        new_buf.shape[1],
    )

    pltpu.make_async_copy(cache, kv_buf, kv_sem).wait()
    rows = attend(
        query[...],
        own[...],
        lambda r: kv_buf[4 * r : 4 * r + 4].reshape(4 * kv_buf.shape[1], 2 * HD),
        lambda r: lengths[r],
        4 * kv_buf.shape[1],
    )
    attended = jnp.concatenate([rows, new_rows], axis=0)
    weight_copy.wait()

    def block_of(shift):
        return pl.ds(pl.multiple_of((z + shift + NZ) % NZ * width, 128), width)

    def part(shift):
        return jnp.dot(attended, weight[:, block_of(shift)], preferred_element_type=jnp.float32)

    two_up[: 2 * REQ] = part(2).astype(jnp.bfloat16)
    two_up[2 * REQ :] = part(3).astype(jnp.bfloat16)
    two_down[: 2 * REQ] = part(-2).astype(jnp.bfloat16)
    two_down[2 * REQ :] = part(-3).astype(jnp.bfloat16)
    opposite[...] = part(4).astype(jnp.bfloat16)
    one_up[...] = part(1)
    one_down[...] = part(-1)
    columns = block_of(0)
    block = jnp.concatenate([resid[:, columns], new_resid[:, columns]], axis=0)
    first[...] = part(0) + jnp.where(x_lo == 0, block.astype(jnp.float32), 0.0)

    me = group_index()
    for j in range(REQ):
        count[j] = 0
    row = lax.broadcasted_iota(jnp.int32, (2 * REQ, REQ), 0)
    column = lax.broadcasted_iota(jnp.int32, (2 * REQ, REQ), 1)
    target_row = jnp.zeros((2 * REQ, REQ), jnp.int32)
    for i in range(REQ):
        target = pairing[i]
        k = count[target]
        count[target] = k + 1
        target_row = jnp.where(column == i, (me ^ target) * 2 + k, target_row)
    chosen[...] = jnp.where(row == target_row, 1.0, 0.0).astype(jnp.bfloat16)


def front(*args):
    pairing, lengths, table, new_lengths, query, own, new_query, new_own, resid, new_resid, weight, new_cache, cache = args
    width = weight.shape[1] // NZ
    any_space = pl.BlockSpec(memory_space=pltpu.HBM)
    vmem = pl.BlockSpec(memory_space=VMEM)
    return pl.pallas_call(
        front_kernel,
        out_shape=[jax.ShapeDtypeStruct((2 * REQ, width), jnp.float32)] * 3
        + [jax.ShapeDtypeStruct((4 * REQ, width), jnp.bfloat16)] * 2
        + [jax.ShapeDtypeStruct((2 * REQ, width), jnp.bfloat16)]
        + [jax.ShapeDtypeStruct((2 * REQ, REQ), jnp.bfloat16)],
        in_specs=[any_space] * 13,
        out_specs=[vmem] * 7,
        scratch_shapes=[SMEM(array.shape, array.dtype) for array in args[:4]]
        + [VMEM(array.shape, array.dtype) for array in args[4:12]]
        + [
            VMEM(cache.shape, jnp.bfloat16),
            SMEM((REQ,), jnp.int32),
            pltpu.SemaphoreType.DMA,
            pltpu.SemaphoreType.DMA((10,)),
            pltpu.SemaphoreType.DMA,
            pltpu.SemaphoreType.DMA,
            pltpu.SemaphoreType.DMA,
        ],
        compiler_params=pltpu.CompilerParams(vmem_limit_bytes=VMEM_LIMIT - 2560 * 1024),
        cost_estimate=pl.CostEstimate(
            flops=400_000_000, bytes_accessed=9_500_000, transcendentals=30_000
        ),
        name="front",
    )(*args)


def spread_kernel(first, *refs):
    *parts, chosen, near, far = refs
    total = first[...]
    for part in parts:
        total = total + part[: 2 * REQ].astype(jnp.float32)
    half = total.astype(jnp.bfloat16)
    placed = jnp.dot(chosen[...], half[REQ:], preferred_element_type=jnp.float32)
    placed = placed.astype(jnp.bfloat16)
    near[:REQ] = half[:REQ]
    near[REQ:] = placed[:REQ]
    far[...] = placed[REQ:]


def finish_kernel(gain, *refs):
    *blocks, hidden, normed = refs
    z, me = lax.axis_index("tp") // 2, group_index()
    rows, width = blocks[0].shape
    slots = rows - REQ
    slot = lax.broadcasted_iota(jnp.int32, (slots, slots), 0)
    column = lax.broadcasted_iota(jnp.int32, (slots, slots), 1)
    offset = (slot >> 1) ^ me
    at = (offset & 1) * 16 + ((offset >> 1) & 3) * 4 + (offset >> 3) * 2 + (slot & 1)
    order = jnp.where(column == at, 1.0, 0.0).astype(jnp.bfloat16)
    square = jnp.zeros((rows, 1), jnp.float32)
    places = [(0, 0, 0), (1, 0, -1), (2, 0, 1), (3, 0, 4), (4, 0, -2), (4, 1, -3), (5, 0, 2), (5, 1, 3)]
    for n, part, shift in places:
        columns = pl.ds(pl.multiple_of((z + shift + NZ) % NZ * width, 128), width)
        block = blocks[n][rows * part : rows * (part + 1)]
        placed = jnp.dot(order, block[REQ:], preferred_element_type=jnp.float32)
        wide = jnp.concatenate([block[:REQ].astype(jnp.float32), placed], axis=0)
        hidden[:, columns] = wide.astype(jnp.bfloat16)
        square = square + jnp.sum(wide * wide, axis=-1, keepdims=True)
    inverse = lax.rsqrt(square / (width * NZ) + 1e-06)
    for k in range(NZ):
        columns = slice(k * width, (k + 1) * width)
        wide = hidden[:, columns].astype(jnp.float32)
        normed[:, columns] = (wide * inverse * gain[:, columns].astype(jnp.float32)).astype(
            jnp.bfloat16
        )


def place_kernel(start, part, *refs):
    whole, buf, in_sem, out_sem = refs[-4:]
    size = part.shape[0] // 4
    for n in range(4):
        rows = pl.ds(n * size, size)
        pltpu.make_async_copy(part.at[rows], buf.at[rows], in_sem.at[n]).start()
    for n in range(4):
        rows = pl.ds(n * size, size)
        pltpu.make_async_copy(part.at[rows], buf.at[rows], in_sem.at[n]).wait()
        target = whole.at[rows, pl.ds(start, part.shape[1])]
        pltpu.make_async_copy(buf.at[rows], target, out_sem.at[n]).start()
    for n in range(4):
        rows = pl.ds(n * size, size)
        target = whole.at[rows, pl.ds(start, part.shape[1])]
        pltpu.make_async_copy(buf.at[rows], target, out_sem.at[n]).wait()


def place(part, start, whole):
    given = [part] if isinstance(whole, tuple) else [part, whole]
    shape = whole if isinstance(whole, tuple) else whole.shape
    any_space = pl.BlockSpec(memory_space=pltpu.HBM)
    return pl.pallas_call(
        functools.partial(place_kernel, start),
        out_shape=jax.ShapeDtypeStruct(shape, part.dtype),
        in_specs=[any_space] * len(given),
        out_specs=any_space,
        scratch_shapes=[
            VMEM(part.shape, part.dtype),
            pltpu.SemaphoreType.DMA((4,)),
            pltpu.SemaphoreType.DMA((4,)),
        ],
        compiler_params=pltpu.CompilerParams(vmem_limit_bytes=SMALL_LIMIT),
        input_output_aliases={} if len(given) == 1 else {1: 0},
        cost_estimate=pl.CostEstimate(flops=0, bytes_accessed=2 * part.size * 2, transcendentals=0),
        name="place",
    )(*given)


def body(
    cache,
    table,
    lengths,
    query,
    step_kv,
    resid,
    new_cache,
    new_lengths,
    new_query,
    new_step_kv,
    new_resid,
    pairing,
    o_weight,
    norm_gain,
):
    pools, groups = lax.axis_size("pool"), lax.axis_size("pool") * lax.axis_size("group")
    ranks = lax.axis_size("tp")
    pair = pairing[0, 0, :, 0]
    prompts = new_cache[0, 0, :, :, 0]
    vmem = pl.BlockSpec(memory_space=VMEM)
    both = ("pool", "group")

    def over_tp(array, flip):
        return lax.ppermute(array, "tp", [(t, t ^ flip) for t in range(ranks)])

    def round_z(array, shift):
        return lax.ppermute(array, "tp", [(t, (t + 2 * shift) % ranks) for t in range(ranks)])

    def over_groups(array, flip):
        return lax.ppermute(array, both, [(s, s ^ flip) for s in range(groups)])

    def deliver(array):
        blocks = array.reshape((groups, 2) + array.shape[1:])
        return lax.all_to_all(blocks, both, split_axis=0, concat_axis=0, tiled=True).reshape(array.shape)

    early, late = pack(pair, new_lengths[0, 0], new_step_kv[0, 0, :, 0], prompts)
    early = deliver(early)

    first, one_up, one_down, two_up, two_down, opposite, chosen = front(
        pair,
        lengths[0, 0],
        table[0, 0],
        new_lengths[0, 0],
        query[0, 0],
        step_kv[0, 0, :, 0],
        new_query[0, 0],
        new_step_kv[0, 0, :, 0],
        resid[0, 0],
        new_resid[0, 0],
        o_weight,
        prompts,
        cache[0, 0, :, :, 0],
    )
    from_below, from_above = round_z(two_up, 2), round_z(two_down, -2)
    opposite = round_z(opposite, 4)
    gain = norm_gain.reshape(1, -1)
    from_below, from_above, opposite, gain = lax.optimization_barrier(
        (from_below, from_above, opposite, gain)
    )
    one_up = (one_up + from_below[2 * REQ :].astype(jnp.float32)).astype(jnp.bfloat16)
    one_down = (one_down + from_above[2 * REQ :].astype(jnp.float32)).astype(jnp.bfloat16)
    parts = [from_below, from_above, opposite, round_z(one_up, 1), round_z(one_down, -1)]
    width = first.shape[1]
    near, far = pl.pallas_call(
        spread_kernel,
        out_shape=[
            jax.ShapeDtypeStruct((2 * REQ, width), jnp.bfloat16),
            jax.ShapeDtypeStruct((REQ, width), jnp.bfloat16),
        ],
        in_specs=[vmem] * (len(parts) + 2),
        out_specs=[vmem] * 2,
        compiler_params=pltpu.CompilerParams(vmem_limit_bytes=SMALL_LIMIT),
        name="spread",
    )(first, *parts, chosen)

    across = [(n, n ^ (ranks + 1)) for n in range(pools * ranks)]
    far_here = over_groups(far, groups // 2)
    far_there = lax.ppermute(far, ("pool", "tp"), across)
    near_there = over_tp(near, 1)
    near = (near.astype(jnp.float32) + near_there.astype(jnp.float32)).astype(jnp.bfloat16)
    far = (far_here.astype(jnp.float32) + far_there.astype(jnp.float32)).astype(jnp.bfloat16)
    toward = [
        jnp.concatenate([near[REQ + 4 * y : REQ + 4 * y + 4], far[4 * y : 4 * y + 4]], axis=0)
        for y in range(4)
    ]
    slots = [toward[0]] + [over_groups(toward[y], 2 * y) for y in range(1, 4)]
    late, *slots = lax.optimization_barrier((late, *slots))
    late = deliver(late)
    slots = jnp.stack(slots).reshape(4, 2, 2, 2, width)
    kept, given = (slots[:, :, c].reshape(REQ, width) for c in range(2))
    block = jnp.concatenate([near[:REQ], kept, over_groups(given, 1)], axis=0)

    slot_cache = place(early, 0, (2 * REQ,) + prompts.shape[1:])
    below, above, opposite, slot_cache = lax.optimization_barrier(
        (round_z(block, 1), round_z(block, -1), round_z(block, 4), slot_cache)
    )
    two_below = round_z(jnp.concatenate([block, below], axis=0), 2)
    two_above = round_z(jnp.concatenate([block, above], axis=0), -2)
    blocks = [block, below, above, opposite, two_below, two_above]
    hidden, normed = pl.pallas_call(
        finish_kernel,
        out_shape=[jax.ShapeDtypeStruct((block.shape[0], width * NZ), jnp.bfloat16)] * 2,
        in_specs=[vmem] * (len(blocks) + 1),
        out_specs=[vmem] * 2,
        compiler_params=pltpu.CompilerParams(vmem_limit_bytes=SMALL_LIMIT),
        name="finish",
    )(gain, *blocks)

    slot_cache = place(late, CUT, slot_cache)
    return (hidden[None, None], normed[None, None], slot_cache[None, None, :, :, None, :])


def solution(mesh):
    placed = (
        P("pool", "group", None, None, "tp", None),
        P("pool", "group", None),
        P("pool", "group", None),
        P("pool", "group", None, "tp"),
        P("pool", "group", None, "tp", None),
        P("pool", "group", None, None),
        P("pool", "group", None, None, "tp", None),
        P("pool", "group", None),
        P("pool", "group", None, "tp"),
        P("pool", "group", None, "tp", None),
        P("pool", "group", None, None),
        P("pool", "group", None, None),
        P("tp", None),
        P(),
    )
    return jax.shard_map(
        body,
        mesh=mesh,
        in_specs=placed,
        out_specs=(
            P("pool", "group", None, None),
            P("pool", "group", None, None),
            P("pool", "group", None, None, "tp", None),
        ),
        check_vma=False,
    )
```

```python
import functools
import math

import jax
import jax.numpy as jnp
from jax import lax
from jax.experimental import pallas as pl
from jax.experimental.pallas import tpu as pltpu
from jax.sharding import PartitionSpec as P

REQ = 16
HD = 128
NZ = 8
CUT = 160
SMEM = pltpu.SMEM
VMEM = pltpu.VMEM
VMEM_LIMIT = 63 * 1024 * 1024
FRONT_LIMIT = 52 * 1024 * 1024
SMALL_LIMIT = 8 * 1024 * 1024


def softmax_parts(scores, own_score, lengths):
    position = lax.broadcasted_iota(jnp.int32, scores.shape, 1)
    visible = position < lengths
    top = jnp.max(jnp.where(visible, scores, -1e30), axis=-1, keepdims=True)
    top = jnp.maximum(top, own_score)
    exponent = jnp.where(visible, jnp.exp(scores - top), 0.0)
    own_exponent = jnp.exp(own_score - top)
    denominator = jnp.sum(exponent, axis=-1, keepdims=True) + own_exponent
    weights = (exponent / denominator).astype(jnp.bfloat16).astype(jnp.float32)
    own_weight = (own_exponent / denominator).astype(jnp.bfloat16).astype(jnp.float32)
    return weights, own_weight


def heads_as_rows(wide):
    return jnp.concatenate([wide[:, :HD], wide[:, HD:]], axis=0)


def attend(query, own, kv_of, length_of, tokens):
    rows = 2 * REQ
    scale = 1.0 / math.sqrt(HD)
    heads = heads_as_rows(query)
    own_key = own[:, :HD].astype(jnp.float32)
    own_value = own[:, HD:].astype(jnp.float32)
    own_key = jnp.concatenate([own_key, own_key], axis=0)
    own_value = jnp.concatenate([own_value, own_value], axis=0)
    own_score = jnp.sum(heads.astype(jnp.float32) * own_key, axis=-1, keepdims=True) * scale
    request = lax.broadcasted_iota(jnp.int32, (rows, 1), 0) % REQ
    lengths = jnp.zeros((rows, 1), jnp.int32)
    scores = jnp.zeros((rows, tokens), jnp.float32)
    for r in range(REQ):
        lengths = jnp.where(request == r, length_of(r), lengths)
        one = lax.dot_general(
            heads, kv_of(r)[:, :HD], (((1,), (1,)), ((), ())), preferred_element_type=jnp.float32
        )
        scores = jnp.where(request == r, one, scores)
    weights, own_weight = softmax_parts(scores * scale, own_score, lengths)
    total = own_weight * own_value
    for r in range(REQ):
        mine = jnp.where(request == r, weights, 0.0).astype(jnp.bfloat16)
        total = total + jnp.dot(mine, kv_of(r)[:, HD:], preferred_element_type=jnp.float32)
    attended = total.astype(jnp.bfloat16)
    return jnp.concatenate([attended[:REQ], attended[REQ:]], axis=1)


def group_index():
    return lax.axis_index("pool") * lax.axis_size("group") + lax.axis_index("group")


def pack_kernel(pairing_in, lengths_in, own_in, new_cache, early, late, buf, own, pairing, lengths, taken, count, small_sem, in_sem, early_sem, late_sem):
    small = [
        pltpu.make_async_copy(pairing_in, pairing, small_sem.at[0]),
        pltpu.make_async_copy(lengths_in, lengths, small_sem.at[1]),
        pltpu.make_async_copy(own_in, own, small_sem.at[2]),
    ]
    for copy in small:
        copy.start()
    load = pltpu.make_async_copy(new_cache, buf.at[pl.ds(0, REQ)], in_sem)
    load.start()
    buf[REQ] = jnp.zeros(buf.shape[1:], buf.dtype)
    for j in range(2 * REQ):
        taken[j] = REQ
    for j in range(REQ):
        count[j] = 0
    for copy in small:
        copy.wait()
    for i in range(REQ):
        target = pairing[i]
        k = count[target]
        count[target] = k + 1
        taken[2 * target + k] = i
    row = lax.broadcasted_iota(jnp.int32, (16, 1), 0)
    load.wait()
    for i in range(REQ):
        base = pl.multiple_of(lengths[i] // 16 * 16, 16)
        window = buf[i, pl.ds(base, 16), :].astype(jnp.float32)
        token = own[i : i + 1, :].astype(jnp.float32)
        window = jnp.where(row == lengths[i] - base, token, window)
        buf[i, pl.ds(base, 16), :] = window.astype(buf.dtype)
    cut = early.shape[1]
    for j in range(2 * REQ):
        request = buf.at[taken[j]]
        pltpu.make_async_copy(request.at[pl.ds(0, cut)], early.at[j], early_sem).start()
    for j in range(2 * REQ):
        request = buf.at[taken[j]]
        pltpu.make_async_copy(request.at[pl.ds(cut, late.shape[1])], late.at[j], late_sem).start()
    pltpu.make_async_copy(early, early, early_sem).wait()
    pltpu.make_async_copy(late, late, late_sem).wait()


def pack(pairing, new_lengths, new_own, new_cache):
    tokens = new_cache.shape[1]
    any_space = pl.BlockSpec(memory_space=pltpu.HBM)
    return pl.pallas_call(
        pack_kernel,
        out_shape=[
            jax.ShapeDtypeStruct((2 * REQ, CUT, 2 * HD), jnp.bfloat16),
            jax.ShapeDtypeStruct((2 * REQ, tokens - CUT, 2 * HD), jnp.bfloat16),
        ],
        in_specs=[any_space] * 4,
        out_specs=[any_space] * 2,
        scratch_shapes=[
            VMEM((REQ + 1, tokens, 2 * HD), jnp.bfloat16),
            VMEM(new_own.shape, jnp.bfloat16),
            SMEM((REQ,), jnp.int32),
            SMEM((REQ,), jnp.int32),
            SMEM((2 * REQ,), jnp.int32),
            SMEM((REQ,), jnp.int32),
            pltpu.SemaphoreType.DMA((3,)),
            pltpu.SemaphoreType.DMA,
            pltpu.SemaphoreType.DMA,
            pltpu.SemaphoreType.DMA,
        ],
        compiler_params=pltpu.CompilerParams(vmem_limit_bytes=VMEM_LIMIT),
        cost_estimate=pl.CostEstimate(flops=1_000_000, bytes_accessed=6_400_000, transcendentals=0),
        name="pack",
    )(pairing, new_lengths, new_own, new_cache)


def front_kernel(*refs):
    ins, refs = refs[:13], refs[13:]
    first, one_up, one_down, two_up, two_down, opposite, chosen = refs[:7]
    refs = refs[7:]
    bufs, (count, table_sem, small_sem, new_sem, kv_sem, weight_sem) = refs[:13], refs[13:]
    pairing, lengths, table, new_lengths, query, own, new_query, new_own, resid, new_resid, weight, new_buf, kv_buf = bufs
    new_cache, cache = ins[11], ins[12]
    z, x_lo = lax.axis_index("tp") // 2, lax.axis_index("tp") % 2
    width = weight.shape[1] // NZ

    table_copy = pltpu.make_async_copy(ins[2], table, table_sem)
    table_copy.start()
    small = [pltpu.make_async_copy(ins[n], bufs[n], small_sem.at[n]) for n in range(10) if n != 2]
    new_copy = pltpu.make_async_copy(new_cache, new_buf, new_sem)
    weight_copy = pltpu.make_async_copy(ins[10], weight, weight_sem)
    for copy in small:
        copy.start()
    new_copy.start()
    table_copy.wait()
    for e in range(4 * REQ):
        pltpu.make_async_copy(cache.at[table[e]], kv_buf.at[e], kv_sem).start()
    weight_copy.start()
    for copy in small:
        copy.wait()
    new_copy.wait()

    new_rows = attend(
        new_query[...],
        new_own[...],
        lambda r: new_buf[r],
        lambda r: new_lengths[r],
        new_buf.shape[1],
    )

    pltpu.make_async_copy(cache, kv_buf, kv_sem).wait()
    rows = attend(
        query[...],
        own[...],
        lambda r: kv_buf[4 * r : 4 * r + 4].reshape(4 * kv_buf.shape[1], 2 * HD),
        lambda r: lengths[r],
        4 * kv_buf.shape[1],
    )
    attended = jnp.concatenate([rows, new_rows], axis=0)
    weight_copy.wait()

    def block_of(shift):
        return pl.ds(pl.multiple_of((z + shift + NZ) % NZ * width, 128), width)

    def part(shift):
        return jnp.dot(attended, weight[:, block_of(shift)], preferred_element_type=jnp.float32)

    two_up[: 2 * REQ] = part(2).astype(jnp.bfloat16)
    two_up[2 * REQ :] = part(3).astype(jnp.bfloat16)
    two_down[: 2 * REQ] = part(-2).astype(jnp.bfloat16)
    two_down[2 * REQ :] = part(-3).astype(jnp.bfloat16)
    opposite[...] = part(4).astype(jnp.bfloat16)
    one_up[...] = part(1)
    one_down[...] = part(-1)
    columns = block_of(0)
    block = jnp.concatenate([resid[:, columns], new_resid[:, columns]], axis=0)
    first[...] = part(0) + jnp.where(x_lo == 0, block.astype(jnp.float32), 0.0)

    me = group_index()
    for j in range(REQ):
        count[j] = 0
    row = lax.broadcasted_iota(jnp.int32, (2 * REQ, REQ), 0)
    column = lax.broadcasted_iota(jnp.int32, (2 * REQ, REQ), 1)
    target_row = jnp.zeros((2 * REQ, REQ), jnp.int32)
    for i in range(REQ):
        target = pairing[i]
        k = count[target]
        count[target] = k + 1
        target_row = jnp.where(column == i, (me ^ target) * 2 + k, target_row)
    chosen[...] = jnp.where(row == target_row, 1.0, 0.0).astype(jnp.bfloat16)


def front(*args):
    pairing, lengths, table, new_lengths, query, own, new_query, new_own, resid, new_resid, weight, new_cache, cache = args
    width = weight.shape[1] // NZ
    any_space = pl.BlockSpec(memory_space=pltpu.HBM)
    vmem = pl.BlockSpec(memory_space=VMEM)
    return pl.pallas_call(
        front_kernel,
        out_shape=[jax.ShapeDtypeStruct((2 * REQ, width), jnp.float32)] * 3
        + [jax.ShapeDtypeStruct((4 * REQ, width), jnp.bfloat16)] * 2
        + [jax.ShapeDtypeStruct((2 * REQ, width), jnp.bfloat16)]
        + [jax.ShapeDtypeStruct((2 * REQ, REQ), jnp.bfloat16)],
        in_specs=[any_space] * 13,
        out_specs=[vmem] * 7,
        scratch_shapes=[SMEM(array.shape, array.dtype) for array in args[:4]]
        + [VMEM(array.shape, array.dtype) for array in args[4:12]]
        + [
            VMEM(cache.shape, jnp.bfloat16),
            SMEM((REQ,), jnp.int32),
            pltpu.SemaphoreType.DMA,
            pltpu.SemaphoreType.DMA((10,)),
            pltpu.SemaphoreType.DMA,
            pltpu.SemaphoreType.DMA,
            pltpu.SemaphoreType.DMA,
        ],
        compiler_params=pltpu.CompilerParams(vmem_limit_bytes=FRONT_LIMIT),
        cost_estimate=pl.CostEstimate(
            flops=400_000_000, bytes_accessed=9_500_000, transcendentals=30_000
        ),
        name="front",
    )(*args)


def spread_kernel(first, *refs):
    *parts, chosen, near, far = refs
    total = first[...]
    for part in parts:
        total = total + part[: 2 * REQ].astype(jnp.float32)
    half = total.astype(jnp.bfloat16)
    placed = jnp.dot(chosen[...], half[REQ:], preferred_element_type=jnp.float32)
    placed = placed.astype(jnp.bfloat16)
    near[:REQ] = half[:REQ]
    near[REQ:] = placed[:REQ]
    far[...] = placed[REQ:]


def finish_kernel(gain, *refs):
    *blocks, hidden, normed = refs
    z, me = lax.axis_index("tp") // 2, group_index()
    rows, width = blocks[0].shape
    slots = rows - REQ
    slot = lax.broadcasted_iota(jnp.int32, (slots, slots), 0)
    column = lax.broadcasted_iota(jnp.int32, (slots, slots), 1)
    offset = (slot >> 1) ^ me
    at = (offset & 1) * 16 + ((offset >> 1) & 3) * 4 + (offset >> 3) * 2 + (slot & 1)
    order = jnp.where(column == at, 1.0, 0.0).astype(jnp.bfloat16)
    square = jnp.zeros((rows, 1), jnp.float32)
    places = [(0, 0, 0), (1, 0, -1), (2, 0, 1), (3, 0, 4), (4, 0, -2), (4, 1, -3), (5, 0, 2), (5, 1, 3)]
    for n, part, shift in places:
        columns = pl.ds(pl.multiple_of((z + shift + NZ) % NZ * width, 128), width)
        block = blocks[n][rows * part : rows * (part + 1)]
        placed = jnp.dot(order, block[REQ:], preferred_element_type=jnp.float32)
        wide = jnp.concatenate([block[:REQ].astype(jnp.float32), placed], axis=0)
        hidden[:, columns] = wide.astype(jnp.bfloat16)
        square = square + jnp.sum(wide * wide, axis=-1, keepdims=True)
    inverse = lax.rsqrt(square / (width * NZ) + 1e-06)
    for k in range(NZ):
        columns = slice(k * width, (k + 1) * width)
        wide = hidden[:, columns].astype(jnp.float32)
        normed[:, columns] = (wide * inverse * gain[:, columns].astype(jnp.float32)).astype(
            jnp.bfloat16
        )


def place_kernel(start, part, *refs):
    whole, buf, in_sem, out_sem = refs[-4:]
    size = part.shape[0] // 4
    for n in range(4):
        rows = pl.ds(n * size, size)
        pltpu.make_async_copy(part.at[rows], buf.at[rows], in_sem.at[n]).start()
    for n in range(4):
        rows = pl.ds(n * size, size)
        pltpu.make_async_copy(part.at[rows], buf.at[rows], in_sem.at[n]).wait()
        target = whole.at[rows, pl.ds(start, part.shape[1])]
        pltpu.make_async_copy(buf.at[rows], target, out_sem.at[n]).start()
    for n in range(4):
        rows = pl.ds(n * size, size)
        target = whole.at[rows, pl.ds(start, part.shape[1])]
        pltpu.make_async_copy(buf.at[rows], target, out_sem.at[n]).wait()


def place(part, start, whole):
    given = [part] if isinstance(whole, tuple) else [part, whole]
    shape = whole if isinstance(whole, tuple) else whole.shape
    any_space = pl.BlockSpec(memory_space=pltpu.HBM)
    return pl.pallas_call(
        functools.partial(place_kernel, start),
        out_shape=jax.ShapeDtypeStruct(shape, part.dtype),
        in_specs=[any_space] * len(given),
        out_specs=any_space,
        scratch_shapes=[
            VMEM(part.shape, part.dtype),
            pltpu.SemaphoreType.DMA((4,)),
            pltpu.SemaphoreType.DMA((4,)),
        ],
        compiler_params=pltpu.CompilerParams(vmem_limit_bytes=SMALL_LIMIT),
        input_output_aliases={} if len(given) == 1 else {1: 0},
        cost_estimate=pl.CostEstimate(flops=0, bytes_accessed=2 * part.size * 2, transcendentals=0),
        name="place",
    )(*given)


def body(
    cache,
    table,
    lengths,
    query,
    step_kv,
    resid,
    new_cache,
    new_lengths,
    new_query,
    new_step_kv,
    new_resid,
    pairing,
    o_weight,
    norm_gain,
):
    pools, groups = lax.axis_size("pool"), lax.axis_size("pool") * lax.axis_size("group")
    ranks = lax.axis_size("tp")
    pair = pairing[0, 0, :, 0]
    prompts = new_cache[0, 0, :, :, 0]
    vmem = pl.BlockSpec(memory_space=VMEM)
    both = ("pool", "group")

    def over_tp(array, flip):
        return lax.ppermute(array, "tp", [(t, t ^ flip) for t in range(ranks)])

    def round_z(array, shift):
        return lax.ppermute(array, "tp", [(t, (t + 2 * shift) % ranks) for t in range(ranks)])

    def over_groups(array, flip):
        return lax.ppermute(array, both, [(s, s ^ flip) for s in range(groups)])

    def deliver(array):
        blocks = array.reshape((groups, 2) + array.shape[1:])
        return lax.all_to_all(blocks, both, split_axis=0, concat_axis=0, tiled=True).reshape(array.shape)

    early, late = pack(pair, new_lengths[0, 0], new_step_kv[0, 0, :, 0], prompts)
    early = deliver(early)

    first, one_up, one_down, two_up, two_down, opposite, chosen = front(
        pair,
        lengths[0, 0],
        table[0, 0],
        new_lengths[0, 0],
        query[0, 0],
        step_kv[0, 0, :, 0],
        new_query[0, 0],
        new_step_kv[0, 0, :, 0],
        resid[0, 0],
        new_resid[0, 0],
        o_weight,
        prompts,
        cache[0, 0, :, :, 0],
    )
    from_below, from_above = round_z(two_up, 2), round_z(two_down, -2)
    opposite = round_z(opposite, 4)
    gain = norm_gain.reshape(1, -1)
    from_below, from_above, opposite, gain = lax.optimization_barrier(
        (from_below, from_above, opposite, gain)
    )
    one_up = (one_up + from_below[2 * REQ :].astype(jnp.float32)).astype(jnp.bfloat16)
    one_down = (one_down + from_above[2 * REQ :].astype(jnp.float32)).astype(jnp.bfloat16)
    parts = [from_below, from_above, opposite, round_z(one_up, 1), round_z(one_down, -1)]
    width = first.shape[1]
    near, far = pl.pallas_call(
        spread_kernel,
        out_shape=[
            jax.ShapeDtypeStruct((2 * REQ, width), jnp.bfloat16),
            jax.ShapeDtypeStruct((REQ, width), jnp.bfloat16),
        ],
        in_specs=[vmem] * (len(parts) + 2),
        out_specs=[vmem] * 2,
        compiler_params=pltpu.CompilerParams(vmem_limit_bytes=SMALL_LIMIT),
        name="spread",
    )(first, *parts, chosen)

    across = [(n, n ^ (ranks + 1)) for n in range(pools * ranks)]
    far_here = over_groups(far, groups // 2)
    far_there = lax.ppermute(far, ("pool", "tp"), across)
    near_there = over_tp(near, 1)
    near = (near.astype(jnp.float32) + near_there.astype(jnp.float32)).astype(jnp.bfloat16)
    far = (far_here.astype(jnp.float32) + far_there.astype(jnp.float32)).astype(jnp.bfloat16)
    toward = [
        jnp.concatenate([near[REQ + 4 * y : REQ + 4 * y + 4], far[4 * y : 4 * y + 4]], axis=0)
        for y in range(4)
    ]
    slots = [toward[0]] + [over_groups(toward[y], 2 * y) for y in range(1, 4)]
    late, *slots = lax.optimization_barrier((late, *slots))
    late = deliver(late)
    slots = jnp.stack(slots).reshape(4, 2, 2, 2, width)
    kept, given = (slots[:, :, c].reshape(REQ, width) for c in range(2))
    block = jnp.concatenate([near[:REQ], kept, over_groups(given, 1)], axis=0)

    slot_cache = place(early, 0, (2 * REQ,) + prompts.shape[1:])
    below, above, opposite, slot_cache = lax.optimization_barrier(
        (round_z(block, 1), round_z(block, -1), round_z(block, 4), slot_cache)
    )
    two_below = round_z(jnp.concatenate([block, below], axis=0), 2)
    two_above = round_z(jnp.concatenate([block, above], axis=0), -2)
    blocks = [block, below, above, opposite, two_below, two_above]
    hidden, normed = pl.pallas_call(
        finish_kernel,
        out_shape=[jax.ShapeDtypeStruct((block.shape[0], width * NZ), jnp.bfloat16)] * 2,
        in_specs=[vmem] * (len(blocks) + 1),
        out_specs=[vmem] * 2,
        compiler_params=pltpu.CompilerParams(vmem_limit_bytes=SMALL_LIMIT),
        name="finish",
    )(gain, *blocks)

    slot_cache = place(late, CUT, slot_cache)
    return (hidden[None, None], normed[None, None], slot_cache[None, None, :, :, None, :])


def solution(mesh):
    placed = (
        P("pool", "group", None, None, "tp", None),
        P("pool", "group", None),
        P("pool", "group", None),
        P("pool", "group", None, "tp"),
        P("pool", "group", None, "tp", None),
        P("pool", "group", None, None),
        P("pool", "group", None, None, "tp", None),
        P("pool", "group", None),
        P("pool", "group", None, "tp"),
        P("pool", "group", None, "tp", None),
        P("pool", "group", None, None),
        P("pool", "group", None, None),
        P("tp", None),
        P(),
    )
    return jax.shard_map(
        body,
        mesh=mesh,
        in_specs=placed,
        out_specs=(
            P("pool", "group", None, None),
            P("pool", "group", None, None),
            P("pool", "group", None, None, "tp", None),
        ),
        check_vma=False,
    )
```

```python
import functools
import math

import jax
import jax.numpy as jnp
from jax import lax
from jax.experimental import pallas as pl
from jax.experimental.pallas import tpu as pltpu
from jax.sharding import PartitionSpec as P

REQ = 16
HD = 128
NZ = 8
CUT = 144
SMEM = pltpu.SMEM
VMEM = pltpu.VMEM
VMEM_LIMIT = 63 * 1024 * 1024
FRONT_LIMIT = 52 * 1024 * 1024
SMALL_LIMIT = 8 * 1024 * 1024


def softmax_parts(scores, own_score, lengths):
    position = lax.broadcasted_iota(jnp.int32, scores.shape, 1)
    visible = position < lengths
    top = jnp.max(jnp.where(visible, scores, -1e30), axis=-1, keepdims=True)
    top = jnp.maximum(top, own_score)
    exponent = jnp.where(visible, jnp.exp(scores - top), 0.0)
    own_exponent = jnp.exp(own_score - top)
    denominator = jnp.sum(exponent, axis=-1, keepdims=True) + own_exponent
    weights = (exponent / denominator).astype(jnp.bfloat16).astype(jnp.float32)
    own_weight = (own_exponent / denominator).astype(jnp.bfloat16).astype(jnp.float32)
    return weights, own_weight


def heads_as_rows(wide):
    return jnp.concatenate([wide[:, :HD], wide[:, HD:]], axis=0)


def attend(query, own, kv_of, length_of, tokens):
    rows = 2 * REQ
    scale = 1.0 / math.sqrt(HD)
    heads = heads_as_rows(query)
    own_key = own[:, :HD].astype(jnp.float32)
    own_value = own[:, HD:].astype(jnp.float32)
    own_key = jnp.concatenate([own_key, own_key], axis=0)
    own_value = jnp.concatenate([own_value, own_value], axis=0)
    own_score = jnp.sum(heads.astype(jnp.float32) * own_key, axis=-1, keepdims=True) * scale
    request = lax.broadcasted_iota(jnp.int32, (rows, 1), 0) % REQ
    lengths = jnp.zeros((rows, 1), jnp.int32)
    scores = jnp.zeros((rows, tokens), jnp.float32)
    for r in range(REQ):
        lengths = jnp.where(request == r, length_of(r), lengths)
        one = lax.dot_general(
            heads, kv_of(r)[:, :HD], (((1,), (1,)), ((), ())), preferred_element_type=jnp.float32
        )
        scores = jnp.where(request == r, one, scores)
    weights, own_weight = softmax_parts(scores * scale, own_score, lengths)
    total = own_weight * own_value
    for r in range(REQ):
        mine = jnp.where(request == r, weights, 0.0).astype(jnp.bfloat16)
        total = total + jnp.dot(mine, kv_of(r)[:, HD:], preferred_element_type=jnp.float32)
    attended = total.astype(jnp.bfloat16)
    return jnp.concatenate([attended[:REQ], attended[REQ:]], axis=1)


def group_index():
    return lax.axis_index("pool") * lax.axis_size("group") + lax.axis_index("group")


def pack_kernel(start, pairing_in, lengths_in, own_in, new_cache, send, buf, own, pairing, lengths, taken, count, small_sem, in_sem, out_sem):
    tokens = send.shape[1]
    small = [
        pltpu.make_async_copy(pairing_in, pairing, small_sem.at[0]),
        pltpu.make_async_copy(lengths_in, lengths, small_sem.at[1]),
        pltpu.make_async_copy(own_in, own, small_sem.at[2]),
    ]
    for copy in small:
        copy.start()
    load = pltpu.make_async_copy(
        new_cache.at[:, pl.ds(start, tokens)], buf.at[pl.ds(0, REQ)], in_sem
    )
    load.start()
    buf[REQ] = jnp.zeros(buf.shape[1:], buf.dtype)
    for j in range(2 * REQ):
        taken[j] = REQ
    for j in range(REQ):
        count[j] = 0
    for copy in small:
        copy.wait()
    for i in range(REQ):
        target = pairing[i]
        k = count[target]
        count[target] = k + 1
        taken[2 * target + k] = i
    row = lax.broadcasted_iota(jnp.int32, (16, 1), 0)
    load.wait()
    for i in range(REQ):
        at = lengths[i] - start

        @pl.when((at >= 0) & (at < tokens))
        def _():
            base = pl.multiple_of(at // 16 * 16, 16)
            window = buf[i, pl.ds(base, 16), :].astype(jnp.float32)
            token = own[i : i + 1, :].astype(jnp.float32)
            window = jnp.where(row == at - base, token, window)
            buf[i, pl.ds(base, 16), :] = window.astype(buf.dtype)

    for j in range(2 * REQ):
        pltpu.make_async_copy(buf.at[taken[j]], send.at[j], out_sem).start()
    pltpu.make_async_copy(send, send, out_sem).wait()


def pack(pairing, new_lengths, new_own, new_cache, start, tokens):
    hbm = pl.BlockSpec(memory_space=pltpu.HBM)
    return pl.pallas_call(
        functools.partial(pack_kernel, start),
        out_shape=jax.ShapeDtypeStruct((2 * REQ, tokens, 2 * HD), jnp.bfloat16),
        in_specs=[hbm] * 4,
        out_specs=hbm,
        scratch_shapes=[
            VMEM((REQ + 1, tokens, 2 * HD), jnp.bfloat16),
            VMEM(new_own.shape, jnp.bfloat16),
            SMEM((REQ,), jnp.int32),
            SMEM((REQ,), jnp.int32),
            SMEM((2 * REQ,), jnp.int32),
            SMEM((REQ,), jnp.int32),
            pltpu.SemaphoreType.DMA((3,)),
            pltpu.SemaphoreType.DMA,
            pltpu.SemaphoreType.DMA,
        ],
        compiler_params=pltpu.CompilerParams(vmem_limit_bytes=VMEM_LIMIT),
        cost_estimate=pl.CostEstimate(flops=0, bytes_accessed=25_000 * tokens, transcendentals=0),
        name="pack",
    )(pairing, new_lengths, new_own, new_cache)


def front_kernel(*refs):
    ins, refs = refs[:13], refs[13:]
    first, one_up, one_down, two_up, two_down, opposite, chosen = refs[:7]
    refs = refs[7:]
    bufs, (count, table_sem, small_sem, new_sem, kv_sem, weight_sem) = refs[:13], refs[13:]
    pairing, lengths, table, new_lengths, query, own, new_query, new_own, resid, new_resid, weight, new_buf, kv_buf = bufs
    new_cache, cache = ins[11], ins[12]
    z, x_lo = lax.axis_index("tp") // 2, lax.axis_index("tp") % 2
    width = weight.shape[1] // NZ

    table_copy = pltpu.make_async_copy(ins[2], table, table_sem)
    table_copy.start()
    small = [pltpu.make_async_copy(ins[n], bufs[n], small_sem.at[n]) for n in range(10) if n != 2]
    new_copy = pltpu.make_async_copy(new_cache, new_buf, new_sem)
    weight_copy = pltpu.make_async_copy(ins[10], weight, weight_sem)
    for copy in small:
        copy.start()
    new_copy.start()
    table_copy.wait()
    for e in range(4 * REQ):
        pltpu.make_async_copy(cache.at[table[e]], kv_buf.at[e], kv_sem).start()
    weight_copy.start()
    for copy in small:
        copy.wait()
    new_copy.wait()

    new_rows = attend(
        new_query[...],
        new_own[...],
        lambda r: new_buf[r],
        lambda r: new_lengths[r],
        new_buf.shape[1],
    )

    pltpu.make_async_copy(cache, kv_buf, kv_sem).wait()
    rows = attend(
        query[...],
        own[...],
        lambda r: kv_buf[4 * r : 4 * r + 4].reshape(4 * kv_buf.shape[1], 2 * HD),
        lambda r: lengths[r],
        4 * kv_buf.shape[1],
    )
    attended = jnp.concatenate([rows, new_rows], axis=0)
    weight_copy.wait()

    def block_of(shift):
        return pl.ds(pl.multiple_of((z + shift + NZ) % NZ * width, 128), width)

    def part(shift):
        return jnp.dot(attended, weight[:, block_of(shift)], preferred_element_type=jnp.float32)

    two_up[: 2 * REQ] = part(2).astype(jnp.bfloat16)
    two_up[2 * REQ :] = part(3).astype(jnp.bfloat16)
    two_down[: 2 * REQ] = part(-2).astype(jnp.bfloat16)
    two_down[2 * REQ :] = part(-3).astype(jnp.bfloat16)
    opposite[...] = part(4).astype(jnp.bfloat16)
    one_up[...] = part(1)
    one_down[...] = part(-1)
    columns = block_of(0)
    block = jnp.concatenate([resid[:, columns], new_resid[:, columns]], axis=0)
    first[...] = part(0) + jnp.where(x_lo == 0, block.astype(jnp.float32), 0.0)

    me = group_index()
    for j in range(REQ):
        count[j] = 0
    row = lax.broadcasted_iota(jnp.int32, (2 * REQ, REQ), 0)
    column = lax.broadcasted_iota(jnp.int32, (2 * REQ, REQ), 1)
    target_row = jnp.zeros((2 * REQ, REQ), jnp.int32)
    for i in range(REQ):
        target = pairing[i]
        k = count[target]
        count[target] = k + 1
        target_row = jnp.where(column == i, (me ^ target) * 2 + k, target_row)
    chosen[...] = jnp.where(row == target_row, 1.0, 0.0).astype(jnp.bfloat16)


def front(*args):
    pairing, lengths, table, new_lengths, query, own, new_query, new_own, resid, new_resid, weight, new_cache, cache = args
    width = weight.shape[1] // NZ
    any_space = pl.BlockSpec(memory_space=pltpu.HBM)
    vmem = pl.BlockSpec(memory_space=VMEM)
    return pl.pallas_call(
        front_kernel,
        out_shape=[jax.ShapeDtypeStruct((2 * REQ, width), jnp.float32)] * 3
        + [jax.ShapeDtypeStruct((4 * REQ, width), jnp.bfloat16)] * 2
        + [jax.ShapeDtypeStruct((2 * REQ, width), jnp.bfloat16)]
        + [jax.ShapeDtypeStruct((2 * REQ, REQ), jnp.bfloat16)],
        in_specs=[any_space] * 13,
        out_specs=[vmem] * 7,
        scratch_shapes=[SMEM(array.shape, array.dtype) for array in args[:4]]
        + [VMEM(array.shape, array.dtype) for array in args[4:12]]
        + [
            VMEM(cache.shape, jnp.bfloat16),
            SMEM((REQ,), jnp.int32),
            pltpu.SemaphoreType.DMA,
            pltpu.SemaphoreType.DMA((10,)),
            pltpu.SemaphoreType.DMA,
            pltpu.SemaphoreType.DMA,
            pltpu.SemaphoreType.DMA,
        ],
        compiler_params=pltpu.CompilerParams(vmem_limit_bytes=FRONT_LIMIT),
        cost_estimate=pl.CostEstimate(
            flops=400_000_000, bytes_accessed=9_500_000, transcendentals=30_000
        ),
        name="front",
    )(*args)


def spread_kernel(first, *refs):
    *parts, chosen, near, far = refs
    total = first[...]
    for part in parts:
        total = total + part[: 2 * REQ].astype(jnp.float32)
    half = total.astype(jnp.bfloat16)
    placed = jnp.dot(chosen[...], half[REQ:], preferred_element_type=jnp.float32)
    placed = placed.astype(jnp.bfloat16)
    near[:REQ] = half[:REQ]
    near[REQ:] = placed[:REQ]
    far[...] = placed[REQ:]


def finish_kernel(gain, *refs):
    *blocks, hidden, normed = refs
    z, me = lax.axis_index("tp") // 2, group_index()
    rows, width = blocks[0].shape
    slots = rows - REQ
    slot = lax.broadcasted_iota(jnp.int32, (slots, slots), 0)
    column = lax.broadcasted_iota(jnp.int32, (slots, slots), 1)
    offset = (slot >> 1) ^ me
    at = (offset & 1) * 16 + ((offset >> 1) & 3) * 4 + (offset >> 3) * 2 + (slot & 1)
    order = jnp.where(column == at, 1.0, 0.0).astype(jnp.bfloat16)
    square = jnp.zeros((rows, 1), jnp.float32)
    places = [(0, 0, 0), (1, 0, -1), (2, 0, 1), (3, 0, 4), (4, 0, -2), (4, 1, -3), (5, 0, 2), (5, 1, 3)]
    for n, part, shift in places:
        columns = pl.ds(pl.multiple_of((z + shift + NZ) % NZ * width, 128), width)
        block = blocks[n][rows * part : rows * (part + 1)]
        placed = jnp.dot(order, block[REQ:], preferred_element_type=jnp.float32)
        wide = jnp.concatenate([block[:REQ].astype(jnp.float32), placed], axis=0)
        hidden[:, columns] = wide.astype(jnp.bfloat16)
        square = square + jnp.sum(wide * wide, axis=-1, keepdims=True)
    inverse = lax.rsqrt(square / (width * NZ) + 1e-06)
    for k in range(NZ):
        columns = slice(k * width, (k + 1) * width)
        wide = hidden[:, columns].astype(jnp.float32)
        normed[:, columns] = (wide * inverse * gain[:, columns].astype(jnp.float32)).astype(
            jnp.bfloat16
        )


def place_kernel(start, part, *refs):
    whole, buf, in_sem, out_sem = refs[-4:]
    size = part.shape[0] // 4
    for n in range(4):
        rows = pl.ds(n * size, size)
        pltpu.make_async_copy(part.at[rows], buf.at[rows], in_sem.at[n]).start()
    for n in range(4):
        rows = pl.ds(n * size, size)
        pltpu.make_async_copy(part.at[rows], buf.at[rows], in_sem.at[n]).wait()
        target = whole.at[rows, pl.ds(start, part.shape[1])]
        pltpu.make_async_copy(buf.at[rows], target, out_sem.at[n]).start()
    for n in range(4):
        rows = pl.ds(n * size, size)
        target = whole.at[rows, pl.ds(start, part.shape[1])]
        pltpu.make_async_copy(buf.at[rows], target, out_sem.at[n]).wait()


def place(part, start, whole):
    given = [part] if isinstance(whole, tuple) else [part, whole]
    shape = whole if isinstance(whole, tuple) else whole.shape
    any_space = pl.BlockSpec(memory_space=pltpu.HBM)
    return pl.pallas_call(
        functools.partial(place_kernel, start),
        out_shape=jax.ShapeDtypeStruct(shape, part.dtype),
        in_specs=[any_space] * len(given),
        out_specs=any_space,
        scratch_shapes=[
            VMEM(part.shape, part.dtype),
            pltpu.SemaphoreType.DMA((4,)),
            pltpu.SemaphoreType.DMA((4,)),
        ],
        compiler_params=pltpu.CompilerParams(vmem_limit_bytes=SMALL_LIMIT),
        input_output_aliases={} if len(given) == 1 else {1: 0},
        cost_estimate=pl.CostEstimate(flops=0, bytes_accessed=2 * part.size * 2, transcendentals=0),
        name="place",
    )(*given)


def body(
    cache,
    table,
    lengths,
    query,
    step_kv,
    resid,
    new_cache,
    new_lengths,
    new_query,
    new_step_kv,
    new_resid,
    pairing,
    o_weight,
    norm_gain,
):
    pools, groups = lax.axis_size("pool"), lax.axis_size("pool") * lax.axis_size("group")
    ranks = lax.axis_size("tp")
    pair = pairing[0, 0, :, 0]
    prompts = new_cache[0, 0, :, :, 0]
    vmem = pl.BlockSpec(memory_space=VMEM)
    both = ("pool", "group")

    def over_tp(array, flip):
        return lax.ppermute(array, "tp", [(t, t ^ flip) for t in range(ranks)])

    def round_z(array, shift):
        return lax.ppermute(array, "tp", [(t, (t + 2 * shift) % ranks) for t in range(ranks)])

    def over_groups(array, flip):
        return lax.ppermute(array, both, [(s, s ^ flip) for s in range(groups)])

    def deliver(array):
        blocks = array.reshape((groups, 2) + array.shape[1:])
        return lax.all_to_all(blocks, both, split_axis=0, concat_axis=0, tiled=True).reshape(array.shape)

    prompt = (pair, new_lengths[0, 0], new_step_kv[0, 0, :, 0], prompts)
    early = deliver(pack(*prompt, 0, CUT))
    late = pack(*prompt, CUT, prompts.shape[1] - CUT)

    first, one_up, one_down, two_up, two_down, opposite, chosen = front(
        pair,
        lengths[0, 0],
        table[0, 0],
        new_lengths[0, 0],
        query[0, 0],
        step_kv[0, 0, :, 0],
        new_query[0, 0],
        new_step_kv[0, 0, :, 0],
        resid[0, 0],
        new_resid[0, 0],
        o_weight,
        prompts,
        cache[0, 0, :, :, 0],
    )
    from_below, from_above = round_z(two_up, 2), round_z(two_down, -2)
    opposite = round_z(opposite, 4)
    gain = norm_gain.reshape(1, -1)
    from_below, from_above, opposite, gain, late = lax.optimization_barrier(
        (from_below, from_above, opposite, gain, late)
    )
    one_up = (one_up + from_below[2 * REQ :].astype(jnp.float32)).astype(jnp.bfloat16)
    one_down = (one_down + from_above[2 * REQ :].astype(jnp.float32)).astype(jnp.bfloat16)
    parts = [from_below, from_above, opposite, round_z(one_up, 1), round_z(one_down, -1)]
    width = first.shape[1]
    near, far = pl.pallas_call(
        spread_kernel,
        out_shape=[
            jax.ShapeDtypeStruct((2 * REQ, width), jnp.bfloat16),
            jax.ShapeDtypeStruct((REQ, width), jnp.bfloat16),
        ],
        in_specs=[vmem] * (len(parts) + 2),
        out_specs=[vmem] * 2,
        compiler_params=pltpu.CompilerParams(vmem_limit_bytes=SMALL_LIMIT),
        name="spread",
    )(first, *parts, chosen)

    across = [(n, n ^ (ranks + 1)) for n in range(pools * ranks)]
    far_here = over_groups(far, groups // 2)
    far_there = lax.ppermute(far, ("pool", "tp"), across)
    near_there = over_tp(near, 1)
    near = (near.astype(jnp.float32) + near_there.astype(jnp.float32)).astype(jnp.bfloat16)
    far = (far_here.astype(jnp.float32) + far_there.astype(jnp.float32)).astype(jnp.bfloat16)
    toward = [
        jnp.concatenate([near[REQ + 4 * y : REQ + 4 * y + 4], far[4 * y : 4 * y + 4]], axis=0)
        for y in range(4)
    ]
    slots = [toward[0]] + [over_groups(toward[y], 2 * y) for y in range(1, 4)]
    late, *slots = lax.optimization_barrier((late, *slots))
    late = deliver(late)
    slots = jnp.stack(slots).reshape(4, 2, 2, 2, width)
    kept, given = (slots[:, :, c].reshape(REQ, width) for c in range(2))
    block = jnp.concatenate([near[:REQ], kept, over_groups(given, 1)], axis=0)

    slot_cache = place(early, 0, (2 * REQ,) + prompts.shape[1:])
    below, above, opposite, slot_cache = lax.optimization_barrier(
        (round_z(block, 1), round_z(block, -1), round_z(block, 4), slot_cache)
    )
    two_below = round_z(jnp.concatenate([block, below], axis=0), 2)
    two_above = round_z(jnp.concatenate([block, above], axis=0), -2)
    blocks = [block, below, above, opposite, two_below, two_above]
    hidden, normed = pl.pallas_call(
        finish_kernel,
        out_shape=[jax.ShapeDtypeStruct((block.shape[0], width * NZ), jnp.bfloat16)] * 2,
        in_specs=[vmem] * (len(blocks) + 1),
        out_specs=[vmem] * 2,
        compiler_params=pltpu.CompilerParams(vmem_limit_bytes=SMALL_LIMIT),
        cost_estimate=pl.CostEstimate(flops=0, bytes_accessed=4_000_000, transcendentals=0),
        name="finish",
    )(gain, *blocks)

    late, hidden = lax.optimization_barrier((late, hidden))
    slot_cache = place(late, CUT, slot_cache)
    return (hidden[None, None], normed[None, None], slot_cache[None, None, :, :, None, :])


def solution(mesh):
    placed = (
        P("pool", "group", None, None, "tp", None),
        P("pool", "group", None),
        P("pool", "group", None),
        P("pool", "group", None, "tp"),
        P("pool", "group", None, "tp", None),
        P("pool", "group", None, None),
        P("pool", "group", None, None, "tp", None),
        P("pool", "group", None),
        P("pool", "group", None, "tp"),
        P("pool", "group", None, "tp", None),
        P("pool", "group", None, None),
        P("pool", "group", None, None),
        P("tp", None),
        P(),
    )
    return jax.shard_map(
        body,
        mesh=mesh,
        in_specs=placed,
        out_specs=(
            P("pool", "group", None, None),
            P("pool", "group", None, None),
            P("pool", "group", None, None, "tp", None),
        ),
        check_vma=False,
    )
```

```python
import functools
import math

import jax
import jax.numpy as jnp
from jax import lax
from jax.experimental import pallas as pl
from jax.experimental.pallas import tpu as pltpu
from jax.sharding import PartitionSpec as P

REQ = 16
HD = 128
NZ = 8
CUT = 144
SMEM = pltpu.SMEM
VMEM = pltpu.VMEM
VMEM_LIMIT = 63 * 1024 * 1024
FRONT_LIMIT = 52 * 1024 * 1024
SMALL_LIMIT = 8 * 1024 * 1024


def softmax_parts(scores, own_score, lengths):
    position = lax.broadcasted_iota(jnp.int32, scores.shape, 1)
    visible = position < lengths
    top = jnp.max(jnp.where(visible, scores, -1e30), axis=-1, keepdims=True)
    top = jnp.maximum(top, own_score)
    exponent = jnp.where(visible, jnp.exp(scores - top), 0.0)
    own_exponent = jnp.exp(own_score - top)
    denominator = jnp.sum(exponent, axis=-1, keepdims=True) + own_exponent
    weights = (exponent / denominator).astype(jnp.bfloat16).astype(jnp.float32)
    own_weight = (own_exponent / denominator).astype(jnp.bfloat16).astype(jnp.float32)
    return weights, own_weight


def heads_as_rows(wide):
    return jnp.concatenate([wide[:, :HD], wide[:, HD:]], axis=0)


def attend(query, own, kv_of, length_of, tokens):
    rows = 2 * REQ
    scale = 1.0 / math.sqrt(HD)
    heads = heads_as_rows(query)
    own_key = own[:, :HD].astype(jnp.float32)
    own_value = own[:, HD:].astype(jnp.float32)
    own_key = jnp.concatenate([own_key, own_key], axis=0)
    own_value = jnp.concatenate([own_value, own_value], axis=0)
    own_score = jnp.sum(heads.astype(jnp.float32) * own_key, axis=-1, keepdims=True) * scale
    request = lax.broadcasted_iota(jnp.int32, (rows, 1), 0) % REQ
    lengths = jnp.zeros((rows, 1), jnp.int32)
    scores = jnp.zeros((rows, tokens), jnp.float32)
    for r in range(REQ):
        lengths = jnp.where(request == r, length_of(r), lengths)
        one = lax.dot_general(
            heads, kv_of(r)[:, :HD], (((1,), (1,)), ((), ())), preferred_element_type=jnp.float32
        )
        scores = jnp.where(request == r, one, scores)
    weights, own_weight = softmax_parts(scores * scale, own_score, lengths)
    total = own_weight * own_value
    for r in range(REQ):
        mine = jnp.where(request == r, weights, 0.0).astype(jnp.bfloat16)
        total = total + jnp.dot(mine, kv_of(r)[:, HD:], preferred_element_type=jnp.float32)
    attended = total.astype(jnp.bfloat16)
    return jnp.concatenate([attended[:REQ], attended[REQ:]], axis=1)


def group_index():
    return lax.axis_index("pool") * lax.axis_size("group") + lax.axis_index("group")


def pack_kernel(start, pairing_in, lengths_in, own_in, new_cache, send, buf, own, pairing, lengths, taken, count, small_sem, in_sem, out_sem):
    tokens = send.shape[1]
    small = [
        pltpu.make_async_copy(pairing_in, pairing, small_sem.at[0]),
        pltpu.make_async_copy(lengths_in, lengths, small_sem.at[1]),
        pltpu.make_async_copy(own_in, own, small_sem.at[2]),
    ]
    for copy in small:
        copy.start()
    load = pltpu.make_async_copy(
        new_cache.at[:, pl.ds(start, tokens)], buf.at[pl.ds(0, REQ)], in_sem
    )
    load.start()
    buf[REQ] = jnp.zeros(buf.shape[1:], buf.dtype)
    for j in range(2 * REQ):
        taken[j] = REQ
    for j in range(REQ):
        count[j] = 0
    for copy in small:
        copy.wait()
    for i in range(REQ):
        target = pairing[i]
        k = count[target]
        count[target] = k + 1
        taken[2 * target + k] = i
    row = lax.broadcasted_iota(jnp.int32, (16, 1), 0)
    load.wait()
    for i in range(REQ):
        at = lengths[i] - start

        @pl.when((at >= 0) & (at < tokens))
        def _():
            base = pl.multiple_of(at // 16 * 16, 16)
            window = buf[i, pl.ds(base, 16), :].astype(jnp.float32)
            token = own[i : i + 1, :].astype(jnp.float32)
            window = jnp.where(row == at - base, token, window)
            buf[i, pl.ds(base, 16), :] = window.astype(buf.dtype)

    for j in range(2 * REQ):
        pltpu.make_async_copy(buf.at[taken[j]], send.at[j], out_sem).start()
    pltpu.make_async_copy(send, send, out_sem).wait()


def pack(pairing, new_lengths, new_own, new_cache, start, tokens):
    hbm = pl.BlockSpec(memory_space=pltpu.HBM)
    return pl.pallas_call(
        functools.partial(pack_kernel, start),
        out_shape=jax.ShapeDtypeStruct((2 * REQ, tokens, 2 * HD), jnp.bfloat16),
        in_specs=[hbm] * 4,
        out_specs=hbm,
        scratch_shapes=[
            VMEM((REQ + 1, tokens, 2 * HD), jnp.bfloat16),
            VMEM(new_own.shape, jnp.bfloat16),
            SMEM((REQ,), jnp.int32),
            SMEM((REQ,), jnp.int32),
            SMEM((2 * REQ,), jnp.int32),
            SMEM((REQ,), jnp.int32),
            pltpu.SemaphoreType.DMA((3,)),
            pltpu.SemaphoreType.DMA,
            pltpu.SemaphoreType.DMA,
        ],
        compiler_params=pltpu.CompilerParams(vmem_limit_bytes=VMEM_LIMIT),
        cost_estimate=pl.CostEstimate(flops=0, bytes_accessed=25_000 * tokens, transcendentals=0),
        name="pack",
    )(pairing, new_lengths, new_own, new_cache)


def front_kernel(*refs):
    ins, refs = refs[:13], refs[13:]
    first, keep_three, send_four, chosen = refs[:4]
    refs = refs[4:]
    bufs, (count, table_sem, small_sem, new_sem, kv_sem, weight_sem) = refs[:13], refs[13:]
    pairing, lengths, table, new_lengths, query, own, new_query, new_own, resid, new_resid, weight, new_buf, kv_buf = bufs
    new_cache, cache = ins[11], ins[12]
    z, x_lo = lax.axis_index("tp") // 2, lax.axis_index("tp") % 2
    width = weight.shape[1] // NZ

    table_copy = pltpu.make_async_copy(ins[2], table, table_sem)
    table_copy.start()
    small = [pltpu.make_async_copy(ins[n], bufs[n], small_sem.at[n]) for n in range(10) if n != 2]
    new_copy = pltpu.make_async_copy(new_cache, new_buf, new_sem)
    weight_copy = pltpu.make_async_copy(ins[10], weight, weight_sem)
    for copy in small:
        copy.start()
    new_copy.start()
    table_copy.wait()
    for e in range(4 * REQ):
        pltpu.make_async_copy(cache.at[table[e]], kv_buf.at[e], kv_sem).start()
    weight_copy.start()
    for copy in small:
        copy.wait()
    new_copy.wait()

    new_rows = attend(
        new_query[...],
        new_own[...],
        lambda r: new_buf[r],
        lambda r: new_lengths[r],
        new_buf.shape[1],
    )

    pltpu.make_async_copy(cache, kv_buf, kv_sem).wait()
    rows = attend(
        query[...],
        own[...],
        lambda r: kv_buf[4 * r : 4 * r + 4].reshape(4 * kv_buf.shape[1], 2 * HD),
        lambda r: lengths[r],
        4 * kv_buf.shape[1],
    )
    attended = jnp.concatenate([rows, new_rows], axis=0)
    weight_copy.wait()

    def part(flip):
        columns = pl.ds(pl.multiple_of((z ^ flip) * width, 128), width)
        return jnp.dot(attended, weight[:, columns], preferred_element_type=jnp.float32)

    for n, flip in enumerate((1, 3, 5, 7)):
        send_four[2 * REQ * n : 2 * REQ * (n + 1)] = part(flip).astype(jnp.bfloat16)
    for n, flip in enumerate((2, 4, 6)):
        keep_three[2 * REQ * n : 2 * REQ * (n + 1)] = part(flip)
    columns = pl.ds(pl.multiple_of(z * width, 128), width)
    block = jnp.concatenate([resid[:, columns], new_resid[:, columns]], axis=0)
    first[...] = part(0) + jnp.where(x_lo == 0, block.astype(jnp.float32), 0.0)

    me = group_index()
    for j in range(REQ):
        count[j] = 0
    row = lax.broadcasted_iota(jnp.int32, (2 * REQ, REQ), 0)
    column = lax.broadcasted_iota(jnp.int32, (2 * REQ, REQ), 1)
    target_row = jnp.zeros((2 * REQ, REQ), jnp.int32)
    for i in range(REQ):
        target = pairing[i]
        k = count[target]
        count[target] = k + 1
        target_row = jnp.where(column == i, (me ^ target) * 2 + k, target_row)
    chosen[...] = jnp.where(row == target_row, 1.0, 0.0).astype(jnp.bfloat16)


def front(*args):
    pairing, lengths, table, new_lengths, query, own, new_query, new_own, resid, new_resid, weight, new_cache, cache = args
    width = weight.shape[1] // NZ
    any_space = pl.BlockSpec(memory_space=pltpu.HBM)
    vmem = pl.BlockSpec(memory_space=VMEM)
    return pl.pallas_call(
        front_kernel,
        out_shape=[
            jax.ShapeDtypeStruct((2 * REQ, width), jnp.float32),
            jax.ShapeDtypeStruct((6 * REQ, width), jnp.float32),
            jax.ShapeDtypeStruct((8 * REQ, width), jnp.bfloat16),
            jax.ShapeDtypeStruct((2 * REQ, REQ), jnp.bfloat16),
        ],
        in_specs=[any_space] * 13,
        out_specs=[vmem] * 4,
        scratch_shapes=[SMEM(array.shape, array.dtype) for array in args[:4]]
        + [VMEM(array.shape, array.dtype) for array in args[4:12]]
        + [
            VMEM(cache.shape, jnp.bfloat16),
            SMEM((REQ,), jnp.int32),
            pltpu.SemaphoreType.DMA,
            pltpu.SemaphoreType.DMA((10,)),
            pltpu.SemaphoreType.DMA,
            pltpu.SemaphoreType.DMA,
            pltpu.SemaphoreType.DMA,
        ],
        compiler_params=pltpu.CompilerParams(vmem_limit_bytes=FRONT_LIMIT),
        cost_estimate=pl.CostEstimate(
            flops=400_000_000, bytes_accessed=9_500_000, transcendentals=30_000
        ),
        name="front",
    )(*args)


def spread_kernel(first, *refs):
    *parts, chosen, near, far = refs
    total = first[...]
    for part in parts:
        total = total + part[: 2 * REQ].astype(jnp.float32)
    half = total.astype(jnp.bfloat16)
    placed = jnp.dot(chosen[...], half[REQ:], preferred_element_type=jnp.float32)
    placed = placed.astype(jnp.bfloat16)
    near[:REQ] = half[:REQ]
    near[REQ:] = placed[:REQ]
    far[...] = placed[REQ:]


def finish_kernel(gain, *refs):
    *blocks, hidden, normed = refs
    z, me = lax.axis_index("tp") // 2, group_index()
    rows, width = hidden.shape[0], blocks[0].shape[1]
    slots = rows - REQ
    slot = lax.broadcasted_iota(jnp.int32, (slots, slots), 0)
    column = lax.broadcasted_iota(jnp.int32, (slots, slots), 1)
    offset = (slot >> 1) ^ me
    at = (offset & 1) * 16 + ((offset >> 1) & 3) * 4 + (offset >> 3) * 2 + (slot & 1)
    order = jnp.where(column == at, 1.0, 0.0).astype(jnp.bfloat16)
    square = jnp.zeros((rows, 1), jnp.float32)
    places = [(0, 0, 0), (0, 1, 2), (0, 2, 6), (0, 3, 4), (1, 0, 1), (1, 1, 3), (1, 2, 7), (1, 3, 5)]
    for n, part, shift in places:
        columns = pl.ds(pl.multiple_of((z ^ shift) * width, 128), width)
        block = blocks[n][rows * part : rows * (part + 1)]
        placed = jnp.dot(order, block[REQ:], preferred_element_type=jnp.float32)
        wide = jnp.concatenate([block[:REQ].astype(jnp.float32), placed], axis=0)
        hidden[:, columns] = wide.astype(jnp.bfloat16)
        square = square + jnp.sum(wide * wide, axis=-1, keepdims=True)
    inverse = lax.rsqrt(square / (width * NZ) + 1e-06)
    for k in range(NZ):
        columns = slice(k * width, (k + 1) * width)
        wide = hidden[:, columns].astype(jnp.float32)
        normed[:, columns] = (wide * inverse * gain[:, columns].astype(jnp.float32)).astype(
            jnp.bfloat16
        )


def place_kernel(start, part, *refs):
    whole, sem = refs[-2:]
    size = part.shape[0] // 4
    copies = [
        pltpu.make_async_copy(
            part.at[pl.ds(n * size, size)],
            whole.at[pl.ds(n * size, size), pl.ds(start, part.shape[1])],
            sem.at[n],
        )
        for n in range(4)
    ]
    for copy in copies:
        copy.start()
    for copy in copies:
        copy.wait()


def place(part, start, whole):
    given = [part] if isinstance(whole, tuple) else [part, whole]
    shape = whole if isinstance(whole, tuple) else whole.shape
    any_space = pl.BlockSpec(memory_space=pltpu.HBM)
    return pl.pallas_call(
        functools.partial(place_kernel, start),
        out_shape=jax.ShapeDtypeStruct(shape, part.dtype),
        in_specs=[pl.BlockSpec(memory_space=VMEM)] + [any_space] * (len(given) - 1),
        out_specs=any_space,
        scratch_shapes=[
            pltpu.SemaphoreType.DMA((4,)),
        ],
        compiler_params=pltpu.CompilerParams(vmem_limit_bytes=SMALL_LIMIT),
        input_output_aliases={} if len(given) == 1 else {1: 0},
        cost_estimate=pl.CostEstimate(flops=0, bytes_accessed=2 * part.size * 2, transcendentals=0),
        name="place",
    )(*given)


def body(
    cache,
    table,
    lengths,
    query,
    step_kv,
    resid,
    new_cache,
    new_lengths,
    new_query,
    new_step_kv,
    new_resid,
    pairing,
    o_weight,
    norm_gain,
):
    pools, groups = lax.axis_size("pool"), lax.axis_size("pool") * lax.axis_size("group")
    ranks = lax.axis_size("tp")
    pair = pairing[0, 0, :, 0]
    prompts = new_cache[0, 0, :, :, 0]
    vmem = pl.BlockSpec(memory_space=VMEM)
    both = ("pool", "group")

    def over_tp(array, flip):
        return lax.ppermute(array, "tp", [(t, t ^ flip) for t in range(ranks)])

    def over_groups(array, flip):
        return lax.ppermute(array, both, [(s, s ^ flip) for s in range(groups)])

    def deliver(array):
        blocks = array.reshape((groups, 2) + array.shape[1:])
        return lax.all_to_all(blocks, both, split_axis=0, concat_axis=0, tiled=True).reshape(array.shape)

    prompt = (pair, new_lengths[0, 0], new_step_kv[0, 0, :, 0], prompts)
    early = deliver(pack(*prompt, 0, CUT))
    late = pack(*prompt, CUT, prompts.shape[1] - CUT)

    first, keep_three, send_four, chosen = front(
        pair,
        lengths[0, 0],
        table[0, 0],
        new_lengths[0, 0],
        query[0, 0],
        step_kv[0, 0, :, 0],
        new_query[0, 0],
        new_step_kv[0, 0, :, 0],
        resid[0, 0],
        new_resid[0, 0],
        o_weight,
        prompts,
        cache[0, 0, :, :, 0],
    )
    four, gain, late = lax.optimization_barrier(
        (over_tp(send_four, 2), norm_gain.reshape(1, -1), late)
    )
    parts = [four]
    for n, flip in enumerate((2, 4, 6)):
        summed = keep_three[2 * REQ * n : 2 * REQ * (n + 1)]
        summed = summed + four[2 * REQ * (n + 1) : 2 * REQ * (n + 2)].astype(jnp.float32)
        parts.append(over_tp(summed.astype(jnp.bfloat16), 2 * flip))
    width = first.shape[1]
    near, far = pl.pallas_call(
        spread_kernel,
        out_shape=[
            jax.ShapeDtypeStruct((2 * REQ, width), jnp.bfloat16),
            jax.ShapeDtypeStruct((REQ, width), jnp.bfloat16),
        ],
        in_specs=[vmem] * (len(parts) + 2),
        out_specs=[vmem] * 2,
        compiler_params=pltpu.CompilerParams(vmem_limit_bytes=SMALL_LIMIT),
        name="spread",
    )(first, *parts, chosen)

    across = [(n, n ^ (ranks + 1)) for n in range(pools * ranks)]
    far_here = over_groups(far, groups // 2)
    far_there = lax.ppermute(far, ("pool", "tp"), across)
    near_there = over_tp(near, 1)
    near = (near.astype(jnp.float32) + near_there.astype(jnp.float32)).astype(jnp.bfloat16)
    far = (far_here.astype(jnp.float32) + far_there.astype(jnp.float32)).astype(jnp.bfloat16)
    toward = [
        jnp.concatenate([near[REQ + 4 * y : REQ + 4 * y + 4], far[4 * y : 4 * y + 4]], axis=0)
        for y in range(4)
    ]
    slots = [toward[0]] + [over_groups(toward[y], 2 * y) for y in range(1, 4)]
    late, *slots = lax.optimization_barrier((late, *slots))
    late = deliver(late)
    slots = jnp.stack(slots).reshape(4, 2, 2, 2, width)
    kept, given = (slots[:, :, c].reshape(REQ, width) for c in range(2))
    block = jnp.concatenate([near[:REQ], kept, over_groups(given, 1)], axis=0)

    slot_cache = place(early, 0, (2 * REQ,) + prompts.shape[1:])
    flips = [over_tp(block, 2 * k) for k in (2, 6, 4)]
    *flips, slot_cache = lax.optimization_barrier((*flips, slot_cache))
    four = jnp.concatenate([block, *flips], axis=0)
    blocks = [four, over_tp(four, 2)]
    hidden, normed = pl.pallas_call(
        finish_kernel,
        out_shape=[jax.ShapeDtypeStruct((block.shape[0], width * NZ), jnp.bfloat16)] * 2,
        in_specs=[vmem] * (len(blocks) + 1),
        out_specs=[vmem] * 2,
        compiler_params=pltpu.CompilerParams(vmem_limit_bytes=SMALL_LIMIT),
        cost_estimate=pl.CostEstimate(flops=0, bytes_accessed=4_000_000, transcendentals=0),
        name="finish",
    )(gain, *blocks)

    late, hidden = lax.optimization_barrier((late, hidden))
    slot_cache = place(late, CUT, slot_cache)
    return (hidden[None, None], normed[None, None], slot_cache[None, None, :, :, None, :])


def solution(mesh):
    placed = (
        P("pool", "group", None, None, "tp", None),
        P("pool", "group", None),
        P("pool", "group", None),
        P("pool", "group", None, "tp"),
        P("pool", "group", None, "tp", None),
        P("pool", "group", None, None),
        P("pool", "group", None, None, "tp", None),
        P("pool", "group", None),
        P("pool", "group", None, "tp"),
        P("pool", "group", None, "tp", None),
        P("pool", "group", None, None),
        P("pool", "group", None, None),
        P("tp", None),
        P(),
    )
    return jax.shard_map(
        body,
        mesh=mesh,
        in_specs=placed,
        out_specs=(
            P("pool", "group", None, None),
            P("pool", "group", None, None),
            P("pool", "group", None, None, "tp", None),
        ),
        check_vma=False,
    )
```

```python
import functools
import math

import jax
import jax.numpy as jnp
from jax import lax
from jax.experimental import pallas as pl
from jax.experimental.pallas import tpu as pltpu
from jax.sharding import PartitionSpec as P

REQ = 16
HD = 128
NZ = 8
CUTS = (144, 144)
SMEM = pltpu.SMEM
VMEM = pltpu.VMEM
VMEM_LIMIT = 63 * 1024 * 1024
FRONT_LIMIT = 52 * 1024 * 1024
SMALL_LIMIT = 8 * 1024 * 1024


def softmax_parts(scores, own_score, lengths):
    position = lax.broadcasted_iota(jnp.int32, scores.shape, 1)
    visible = position < lengths
    top = jnp.max(jnp.where(visible, scores, -1e30), axis=-1, keepdims=True)
    top = jnp.maximum(top, own_score)
    exponent = jnp.where(visible, jnp.exp(scores - top), 0.0)
    own_exponent = jnp.exp(own_score - top)
    denominator = jnp.sum(exponent, axis=-1, keepdims=True) + own_exponent
    weights = (exponent / denominator).astype(jnp.bfloat16).astype(jnp.float32)
    own_weight = (own_exponent / denominator).astype(jnp.bfloat16).astype(jnp.float32)
    return weights, own_weight


def heads_as_rows(wide):
    return jnp.concatenate([wide[:, :HD], wide[:, HD:]], axis=0)


def attend(query, own, kv_of, length_of, tokens):
    rows = 2 * REQ
    scale = 1.0 / math.sqrt(HD)
    heads = heads_as_rows(query)
    own_key = own[:, :HD].astype(jnp.float32)
    own_value = own[:, HD:].astype(jnp.float32)
    own_key = jnp.concatenate([own_key, own_key], axis=0)
    own_value = jnp.concatenate([own_value, own_value], axis=0)
    own_score = jnp.sum(heads.astype(jnp.float32) * own_key, axis=-1, keepdims=True) * scale
    request = lax.broadcasted_iota(jnp.int32, (rows, 1), 0) % REQ
    lengths = jnp.zeros((rows, 1), jnp.int32)
    scores = jnp.zeros((rows, tokens), jnp.float32)
    for r in range(REQ):
        lengths = jnp.where(request == r, length_of(r), lengths)
        one = lax.dot_general(
            heads, kv_of(r)[:, :HD], (((1,), (1,)), ((), ())), preferred_element_type=jnp.float32
        )
        scores = jnp.where(request == r, one, scores)
    weights, own_weight = softmax_parts(scores * scale, own_score, lengths)
    total = own_weight * own_value
    for r in range(REQ):
        mine = jnp.where(request == r, weights, 0.0).astype(jnp.bfloat16)
        total = total + jnp.dot(mine, kv_of(r)[:, HD:], preferred_element_type=jnp.float32)
    attended = total.astype(jnp.bfloat16)
    return jnp.concatenate([attended[:REQ], attended[REQ:]], axis=1)


def group_index():
    return lax.axis_index("pool") * lax.axis_size("group") + lax.axis_index("group")


def pieces_of(late, tokens):
    if late:
        return (CUTS[0], 0, tokens - CUTS[0]), (CUTS[1], tokens - CUTS[0], tokens - CUTS[1])
    return (0, 0, CUTS[0]), (0, CUTS[0], CUTS[1])


def pack_kernel(pieces, pairing_in, lengths_in, own_in, new_cache, send, buf, own, pairing, lengths, taken, count, small_sem, in_sem, out_sem):
    first, tokens = pieces[0][0], buf.shape[1]
    small = [
        pltpu.make_async_copy(pairing_in, pairing, small_sem.at[0]),
        pltpu.make_async_copy(lengths_in, lengths, small_sem.at[1]),
        pltpu.make_async_copy(own_in, own, small_sem.at[2]),
    ]
    for copy in small:
        copy.start()
    load = pltpu.make_async_copy(
        new_cache.at[:, pl.ds(first, tokens)], buf.at[pl.ds(0, REQ)], in_sem
    )
    load.start()
    buf[REQ] = jnp.zeros(buf.shape[1:], buf.dtype)
    for j in range(2 * REQ):
        taken[j] = REQ
    for j in range(REQ):
        count[j] = 0
    for copy in small:
        copy.wait()
    for i in range(REQ):
        target = pairing[i]
        k = count[target]
        count[target] = k + 1
        taken[2 * target + k] = i

    def store(j):
        start, row, size = pieces[j % 2]
        source = buf.at[taken[j], pl.ds(start - first, size)]
        pltpu.make_async_copy(source, send.at[j // 2, pl.ds(row, size)], out_sem).start()

    for j in range(2 * REQ):
        pl.when(taken[j] == REQ)(functools.partial(store, j))
    row = lax.broadcasted_iota(jnp.int32, (16, 1), 0)
    load.wait()
    for i in range(REQ):
        at = lengths[i] - first

        @pl.when((at >= 0) & (at < tokens))
        def _():
            base = pl.multiple_of(at // 16 * 16, 16)
            window = buf[i, pl.ds(base, 16), :].astype(jnp.float32)
            token = own[i : i + 1, :].astype(jnp.float32)
            window = jnp.where(row == at - base, token, window)
            buf[i, pl.ds(base, 16), :] = window.astype(buf.dtype)

    for j in range(2 * REQ):
        pl.when(taken[j] < REQ)(functools.partial(store, j))
    pltpu.make_async_copy(send, send, out_sem).wait()


def pack(pairing, new_lengths, new_own, new_cache, late):
    pieces = pieces_of(late, new_cache.shape[1])
    tokens = max(start + size for start, _, size in pieces) - pieces[0][0]
    hbm = pl.BlockSpec(memory_space=pltpu.HBM)
    return pl.pallas_call(
        functools.partial(pack_kernel, pieces),
        out_shape=jax.ShapeDtypeStruct((REQ, pieces[0][2] + pieces[1][2], 2 * HD), jnp.bfloat16),
        in_specs=[hbm] * 4,
        out_specs=hbm,
        scratch_shapes=[
            VMEM((REQ + 1, tokens, 2 * HD), jnp.bfloat16),
            VMEM(new_own.shape, jnp.bfloat16),
            SMEM((REQ,), jnp.int32),
            SMEM((REQ,), jnp.int32),
            SMEM((2 * REQ,), jnp.int32),
            SMEM((REQ,), jnp.int32),
            pltpu.SemaphoreType.DMA((3,)),
            pltpu.SemaphoreType.DMA,
            pltpu.SemaphoreType.DMA,
        ],
        compiler_params=pltpu.CompilerParams(vmem_limit_bytes=VMEM_LIMIT),
        cost_estimate=pl.CostEstimate(flops=0, bytes_accessed=25_000 * tokens, transcendentals=0),
        name="pack",
    )(pairing, new_lengths, new_own, new_cache)


def front_kernel(*refs):
    ins, refs = refs[:13], refs[13:]
    first, keep_three, send_four, chosen = refs[:4]
    refs = refs[4:]
    bufs, (count, table_sem, small_sem, new_sem, kv_sem, weight_sem) = refs[:13], refs[13:]
    pairing, lengths, table, new_lengths, query, own, new_query, new_own, resid, new_resid, weight, new_buf, kv_buf = bufs
    new_cache, cache = ins[11], ins[12]
    z, x_lo = lax.axis_index("tp") // 2, lax.axis_index("tp") % 2
    width = weight.shape[1] // NZ

    table_copy = pltpu.make_async_copy(ins[2], table, table_sem)
    table_copy.start()
    small = [pltpu.make_async_copy(ins[n], bufs[n], small_sem.at[n]) for n in range(10) if n != 2]
    new_copy = pltpu.make_async_copy(new_cache, new_buf, new_sem)
    weight_copy = pltpu.make_async_copy(ins[10], weight, weight_sem)
    for copy in small:
        copy.start()
    new_copy.start()
    table_copy.wait()
    for e in range(4 * REQ):
        pltpu.make_async_copy(cache.at[table[e]], kv_buf.at[e], kv_sem).start()
    weight_copy.start()
    for copy in small:
        copy.wait()
    new_copy.wait()

    new_rows = attend(
        new_query[...],
        new_own[...],
        lambda r: new_buf[r],
        lambda r: new_lengths[r],
        new_buf.shape[1],
    )

    pltpu.make_async_copy(cache, kv_buf, kv_sem).wait()
    rows = attend(
        query[...],
        own[...],
        lambda r: kv_buf[4 * r : 4 * r + 4].reshape(4 * kv_buf.shape[1], 2 * HD),
        lambda r: lengths[r],
        4 * kv_buf.shape[1],
    )
    attended = jnp.concatenate([rows, new_rows], axis=0)
    weight_copy.wait()

    def part(flip):
        columns = pl.ds(pl.multiple_of((z ^ flip) * width, 128), width)
        return jnp.dot(attended, weight[:, columns], preferred_element_type=jnp.float32)

    for n, flip in enumerate((1, 3, 5, 7)):
        send_four[2 * REQ * n : 2 * REQ * (n + 1)] = part(flip).astype(jnp.bfloat16)
    for n, flip in enumerate((2, 4, 6)):
        keep_three[2 * REQ * n : 2 * REQ * (n + 1)] = part(flip)
    columns = pl.ds(pl.multiple_of(z * width, 128), width)
    block = jnp.concatenate([resid[:, columns], new_resid[:, columns]], axis=0)
    first[...] = part(0) + jnp.where(x_lo == 0, block.astype(jnp.float32), 0.0)

    me = group_index()
    for j in range(REQ):
        count[j] = 0
    row = lax.broadcasted_iota(jnp.int32, (2 * REQ, REQ), 0)
    column = lax.broadcasted_iota(jnp.int32, (2 * REQ, REQ), 1)
    target_row = jnp.zeros((2 * REQ, REQ), jnp.int32)
    for i in range(REQ):
        target = pairing[i]
        k = count[target]
        count[target] = k + 1
        target_row = jnp.where(column == i, (me ^ target) * 2 + k, target_row)
    chosen[...] = jnp.where(row == target_row, 1.0, 0.0).astype(jnp.bfloat16)


def front(*args):
    pairing, lengths, table, new_lengths, query, own, new_query, new_own, resid, new_resid, weight, new_cache, cache = args
    width = weight.shape[1] // NZ
    any_space = pl.BlockSpec(memory_space=pltpu.HBM)
    vmem = pl.BlockSpec(memory_space=VMEM)
    return pl.pallas_call(
        front_kernel,
        out_shape=[
            jax.ShapeDtypeStruct((2 * REQ, width), jnp.float32),
            jax.ShapeDtypeStruct((6 * REQ, width), jnp.float32),
            jax.ShapeDtypeStruct((8 * REQ, width), jnp.bfloat16),
            jax.ShapeDtypeStruct((2 * REQ, REQ), jnp.bfloat16),
        ],
        in_specs=[any_space] * 13,
        out_specs=[vmem] * 4,
        scratch_shapes=[SMEM(array.shape, array.dtype) for array in args[:4]]
        + [VMEM(array.shape, array.dtype) for array in args[4:12]]
        + [
            VMEM(cache.shape, jnp.bfloat16),
            SMEM((REQ,), jnp.int32),
            pltpu.SemaphoreType.DMA,
            pltpu.SemaphoreType.DMA((10,)),
            pltpu.SemaphoreType.DMA,
            pltpu.SemaphoreType.DMA,
            pltpu.SemaphoreType.DMA,
        ],
        compiler_params=pltpu.CompilerParams(vmem_limit_bytes=FRONT_LIMIT),
        cost_estimate=pl.CostEstimate(
            flops=400_000_000, bytes_accessed=9_500_000, transcendentals=30_000
        ),
        name="front",
    )(*args)


def spread_kernel(first, *refs):
    *parts, chosen, near, far = refs
    total = first[...]
    for part in parts:
        total = total + part[: 2 * REQ].astype(jnp.float32)
    half = total.astype(jnp.bfloat16)
    placed = jnp.dot(chosen[...], half[REQ:], preferred_element_type=jnp.float32)
    placed = placed.astype(jnp.bfloat16)
    near[:REQ] = half[:REQ]
    near[REQ:] = placed[:REQ]
    far[...] = placed[REQ:]


def finish_kernel(gain, *refs):
    *blocks, hidden, normed = refs
    z, me = lax.axis_index("tp") // 2, group_index()
    rows, width = hidden.shape[0], blocks[0].shape[1]
    slots = rows - REQ
    slot = lax.broadcasted_iota(jnp.int32, (slots, slots), 0)
    column = lax.broadcasted_iota(jnp.int32, (slots, slots), 1)
    offset = (slot >> 1) ^ me
    at = (offset & 1) * 16 + ((offset >> 1) & 3) * 4 + (offset >> 3) * 2 + (slot & 1)
    order = jnp.where(column == at, 1.0, 0.0).astype(jnp.bfloat16)
    square = jnp.zeros((rows, 1), jnp.float32)
    places = [(0, 0, 0), (0, 1, 2), (0, 2, 6), (0, 3, 4), (1, 0, 1), (1, 1, 3), (1, 2, 7), (1, 3, 5)]
    for n, part, shift in places:
        columns = pl.ds(pl.multiple_of((z ^ shift) * width, 128), width)
        block = blocks[n][rows * part : rows * (part + 1)]
        placed = jnp.dot(order, block[REQ:], preferred_element_type=jnp.float32)
        wide = jnp.concatenate([block[:REQ].astype(jnp.float32), placed], axis=0)
        hidden[:, columns] = wide.astype(jnp.bfloat16)
        square = square + jnp.sum(wide * wide, axis=-1, keepdims=True)
    inverse = lax.rsqrt(square / (width * NZ) + 1e-06)
    for k in range(NZ):
        columns = slice(k * width, (k + 1) * width)
        wide = hidden[:, columns].astype(jnp.float32)
        normed[:, columns] = (wide * inverse * gain[:, columns].astype(jnp.float32)).astype(
            jnp.bfloat16
        )


def place_kernel(pieces, part, *refs):
    whole, sem = refs[-2:]
    size = part.shape[0] // 4
    copies = []
    for n in range(4):
        for k in range(2):
            start, row, tokens = pieces[k]
            groups = pl.ds(n * size, size)
            source = part.at[groups, pl.ds(row, tokens)]
            target = whole.at[groups, k, pl.ds(start, tokens)]
            copies.append(pltpu.make_async_copy(source, target, sem.at[2 * n + k]))
    for copy in copies:
        copy.start()
    for copy in copies:
        copy.wait()


def place(part, late, whole):
    given = [part] if isinstance(whole, tuple) else [part, whole]
    shape = whole if isinstance(whole, tuple) else whole.shape
    hbm = pl.BlockSpec(memory_space=pltpu.HBM)
    return pl.pallas_call(
        functools.partial(place_kernel, pieces_of(late, shape[2])),
        out_shape=jax.ShapeDtypeStruct(shape, part.dtype),
        in_specs=[pl.BlockSpec(memory_space=VMEM)] + [hbm] * (len(given) - 1),
        out_specs=hbm,
        scratch_shapes=[pltpu.SemaphoreType.DMA((8,))],
        compiler_params=pltpu.CompilerParams(vmem_limit_bytes=SMALL_LIMIT),
        input_output_aliases={} if len(given) == 1 else {1: 0},
        cost_estimate=pl.CostEstimate(flops=0, bytes_accessed=2 * part.size * 2, transcendentals=0),
        name="place",
    )(*given)


def body(
    cache,
    table,
    lengths,
    query,
    step_kv,
    resid,
    new_cache,
    new_lengths,
    new_query,
    new_step_kv,
    new_resid,
    pairing,
    o_weight,
    norm_gain,
):
    pools, groups = lax.axis_size("pool"), lax.axis_size("pool") * lax.axis_size("group")
    ranks = lax.axis_size("tp")
    pair = pairing[0, 0, :, 0]
    prompts = new_cache[0, 0, :, :, 0]
    vmem = pl.BlockSpec(memory_space=VMEM)
    both = ("pool", "group")

    def over_tp(array, flip):
        return lax.ppermute(array, "tp", [(t, t ^ flip) for t in range(ranks)])

    def over_groups(array, flip):
        return lax.ppermute(array, both, [(s, s ^ flip) for s in range(groups)])

    def deliver(array):
        return lax.all_to_all(array, both, split_axis=0, concat_axis=0, tiled=True)

    prompt = (pair, new_lengths[0, 0], new_step_kv[0, 0, :, 0], prompts)
    early = deliver(pack(*prompt, False))
    late = pack(*prompt, True)

    first, keep_three, send_four, chosen = front(
        pair,
        lengths[0, 0],
        table[0, 0],
        new_lengths[0, 0],
        query[0, 0],
        step_kv[0, 0, :, 0],
        new_query[0, 0],
        new_step_kv[0, 0, :, 0],
        resid[0, 0],
        new_resid[0, 0],
        o_weight,
        prompts,
        cache[0, 0, :, :, 0],
    )
    four, gain, late = lax.optimization_barrier(
        (over_tp(send_four, 2), norm_gain.reshape(1, -1), late)
    )
    parts = [four]
    for n, flip in ((0, 2), (2, 6), (1, 4)):
        summed = keep_three[2 * REQ * n : 2 * REQ * (n + 1)]
        summed = summed + four[2 * REQ * (n + 1) : 2 * REQ * (n + 2)].astype(jnp.float32)
        parts.append(over_tp(summed.astype(jnp.bfloat16), 2 * flip))
    width = first.shape[1]
    near, far = pl.pallas_call(
        spread_kernel,
        out_shape=[
            jax.ShapeDtypeStruct((2 * REQ, width), jnp.bfloat16),
            jax.ShapeDtypeStruct((REQ, width), jnp.bfloat16),
        ],
        in_specs=[vmem] * (len(parts) + 2),
        out_specs=[vmem] * 2,
        compiler_params=pltpu.CompilerParams(vmem_limit_bytes=SMALL_LIMIT),
        name="spread",
    )(first, *parts, chosen)

    across = [(n, n ^ (ranks + 1)) for n in range(pools * ranks)]
    far_here = over_groups(far, groups // 2)
    far_there = lax.ppermute(far, ("pool", "tp"), across)
    near_there = over_tp(near, 1)
    near = (near.astype(jnp.float32) + near_there.astype(jnp.float32)).astype(jnp.bfloat16)
    far = (far_here.astype(jnp.float32) + far_there.astype(jnp.float32)).astype(jnp.bfloat16)
    toward = [
        jnp.concatenate([near[REQ + 4 * y : REQ + 4 * y + 4], far[4 * y : 4 * y + 4]], axis=0)
        for y in range(4)
    ]
    slots = [toward[0]] + [over_groups(toward[y], 2 * y) for y in range(1, 4)]
    late, *slots = lax.optimization_barrier((late, *slots))
    late = deliver(late)
    slots = jnp.stack(slots).reshape(4, 2, 2, 2, width)
    kept, given = (slots[:, :, c].reshape(REQ, width) for c in range(2))
    block = jnp.concatenate([near[:REQ], kept, over_groups(given, 1)], axis=0)

    slot_cache = place(early, False, (groups, 2) + prompts.shape[1:])
    flips = [over_tp(block, 2 * k) for k in (2, 6, 4)]
    *flips, slot_cache = lax.optimization_barrier((*flips, slot_cache))
    four = jnp.concatenate([block, *flips], axis=0)
    blocks = [four, over_tp(four, 2)]
    hidden, normed = pl.pallas_call(
        finish_kernel,
        out_shape=[jax.ShapeDtypeStruct((block.shape[0], width * NZ), jnp.bfloat16)] * 2,
        in_specs=[vmem] * (len(blocks) + 1),
        out_specs=[vmem] * 2,
        compiler_params=pltpu.CompilerParams(vmem_limit_bytes=SMALL_LIMIT),
        cost_estimate=pl.CostEstimate(flops=0, bytes_accessed=4_000_000, transcendentals=0),
        name="finish",
    )(gain, *blocks)

    late, hidden = lax.optimization_barrier((late, hidden))
    slot_cache = place(late, True, slot_cache).reshape((2 * groups,) + prompts.shape[1:])
    return (hidden[None, None], normed[None, None], slot_cache[None, None, :, :, None, :])


def solution(mesh):
    placed = (
        P("pool", "group", None, None, "tp", None),
        P("pool", "group", None),
        P("pool", "group", None),
        P("pool", "group", None, "tp"),
        P("pool", "group", None, "tp", None),
        P("pool", "group", None, None),
        P("pool", "group", None, None, "tp", None),
        P("pool", "group", None),
        P("pool", "group", None, "tp"),
        P("pool", "group", None, "tp", None),
        P("pool", "group", None, None),
        P("pool", "group", None, None),
        P("tp", None),
        P(),
    )
    return jax.shard_map(
        body,
        mesh=mesh,
        in_specs=placed,
        out_specs=(
            P("pool", "group", None, None),
            P("pool", "group", None, None),
            P("pool", "group", None, None, "tp", None),
        ),
        check_vma=False,
    )
```

```python
import functools
import math

import jax
import jax.numpy as jnp
from jax import lax
from jax.experimental import pallas as pl
from jax.experimental.pallas import tpu as pltpu
from jax.sharding import PartitionSpec as P

REQ = 16
HD = 128
NZ = 8
CUTS = (144, 144)
SMEM = pltpu.SMEM
VMEM = pltpu.VMEM
VMEM_LIMIT = 63 * 1024 * 1024
FRONT_LIMIT = 52 * 1024 * 1024
SMALL_LIMIT = 8 * 1024 * 1024


def softmax_parts(scores, own_score, lengths):
    position = lax.broadcasted_iota(jnp.int32, scores.shape, 1)
    visible = position < lengths
    top = jnp.max(jnp.where(visible, scores, -1e30), axis=-1, keepdims=True)
    top = jnp.maximum(top, own_score)
    exponent = jnp.where(visible, jnp.exp(scores - top), 0.0)
    own_exponent = jnp.exp(own_score - top)
    denominator = jnp.sum(exponent, axis=-1, keepdims=True) + own_exponent
    weights = (exponent / denominator).astype(jnp.bfloat16).astype(jnp.float32)
    own_weight = (own_exponent / denominator).astype(jnp.bfloat16).astype(jnp.float32)
    return weights, own_weight


def heads_as_rows(wide):
    return jnp.concatenate([wide[:, :HD], wide[:, HD:]], axis=0)


def attend(query, own, kv_of, length_of, tokens):
    rows = 2 * REQ
    scale = 1.0 / math.sqrt(HD)
    heads = heads_as_rows(query)
    own_key = own[:, :HD].astype(jnp.float32)
    own_value = own[:, HD:].astype(jnp.float32)
    own_key = jnp.concatenate([own_key, own_key], axis=0)
    own_value = jnp.concatenate([own_value, own_value], axis=0)
    own_score = jnp.sum(heads.astype(jnp.float32) * own_key, axis=-1, keepdims=True) * scale
    request = lax.broadcasted_iota(jnp.int32, (rows, 1), 0) % REQ
    lengths = jnp.zeros((rows, 1), jnp.int32)
    scores = jnp.zeros((rows, tokens), jnp.float32)
    for r in range(REQ):
        lengths = jnp.where(request == r, length_of(r), lengths)
        one = lax.dot_general(
            heads, kv_of(r)[:, :HD], (((1,), (1,)), ((), ())), preferred_element_type=jnp.float32
        )
        scores = jnp.where(request == r, one, scores)
    weights, own_weight = softmax_parts(scores * scale, own_score, lengths)
    total = own_weight * own_value
    for r in range(REQ):
        mine = jnp.where(request == r, weights, 0.0).astype(jnp.bfloat16)
        total = total + jnp.dot(mine, kv_of(r)[:, HD:], preferred_element_type=jnp.float32)
    attended = total.astype(jnp.bfloat16)
    return jnp.concatenate([attended[:REQ], attended[REQ:]], axis=1)


def group_index():
    return lax.axis_index("pool") * lax.axis_size("group") + lax.axis_index("group")


def pieces_of(late, tokens):
    if late:
        return (CUTS[0], 0, tokens - CUTS[0]), (CUTS[1], tokens - CUTS[0], tokens - CUTS[1])
    return (0, 0, CUTS[0]), (0, CUTS[0], CUTS[1])


def pack_kernel(pieces, pairing_in, lengths_in, own_in, new_cache, send, buf, own, pairing, lengths, taken, count, small_sem, in_sem, out_sem):
    first, tokens = pieces[0][0], buf.shape[1]
    small = [
        pltpu.make_async_copy(pairing_in, pairing, small_sem.at[0]),
        pltpu.make_async_copy(lengths_in, lengths, small_sem.at[1]),
        pltpu.make_async_copy(own_in, own, small_sem.at[2]),
    ]
    for copy in small:
        copy.start()
    load = pltpu.make_async_copy(
        new_cache.at[:, pl.ds(first, tokens)], buf.at[pl.ds(0, REQ)], in_sem
    )
    load.start()
    buf[REQ] = jnp.zeros(buf.shape[1:], buf.dtype)
    for j in range(2 * REQ):
        taken[j] = REQ
    for j in range(REQ):
        count[j] = 0
    for copy in small:
        copy.wait()
    for i in range(REQ):
        target = pairing[i]
        k = count[target]
        count[target] = k + 1
        taken[2 * target + k] = i

    def store(j):
        start, row, size = pieces[j % 2]
        source = buf.at[taken[j], pl.ds(start - first, size)]
        pltpu.make_async_copy(source, send.at[j // 2, pl.ds(row, size)], out_sem).start()

    for j in range(2 * REQ):
        pl.when(taken[j] == REQ)(functools.partial(store, j))
    row = lax.broadcasted_iota(jnp.int32, (16, 1), 0)
    load.wait()
    for i in range(REQ):
        at = lengths[i] - first

        @pl.when((at >= 0) & (at < tokens))
        def _():
            base = pl.multiple_of(at // 16 * 16, 16)
            window = buf[i, pl.ds(base, 16), :].astype(jnp.float32)
            token = own[i : i + 1, :].astype(jnp.float32)
            window = jnp.where(row == at - base, token, window)
            buf[i, pl.ds(base, 16), :] = window.astype(buf.dtype)

    for j in range(2 * REQ):
        pl.when(taken[j] < REQ)(functools.partial(store, j))
    pltpu.make_async_copy(send, send, out_sem).wait()


def pack(pairing, new_lengths, new_own, new_cache, late):
    pieces = pieces_of(late, new_cache.shape[1])
    tokens = max(start + size for start, _, size in pieces) - pieces[0][0]
    hbm = pl.BlockSpec(memory_space=pltpu.HBM)
    return pl.pallas_call(
        functools.partial(pack_kernel, pieces),
        out_shape=jax.ShapeDtypeStruct((REQ, pieces[0][2] + pieces[1][2], 2 * HD), jnp.bfloat16),
        in_specs=[hbm] * 4,
        out_specs=hbm,
        scratch_shapes=[
            VMEM((REQ + 1, tokens, 2 * HD), jnp.bfloat16),
            VMEM(new_own.shape, jnp.bfloat16),
            SMEM((REQ,), jnp.int32),
            SMEM((REQ,), jnp.int32),
            SMEM((2 * REQ,), jnp.int32),
            SMEM((REQ,), jnp.int32),
            pltpu.SemaphoreType.DMA((3,)),
            pltpu.SemaphoreType.DMA,
            pltpu.SemaphoreType.DMA,
        ],
        compiler_params=pltpu.CompilerParams(vmem_limit_bytes=VMEM_LIMIT),
        cost_estimate=pl.CostEstimate(flops=0, bytes_accessed=25_000 * tokens, transcendentals=0),
        name="pack",
    )(pairing, new_lengths, new_own, new_cache)


def front_kernel(*refs):
    ins, refs = refs[:13], refs[13:]
    first, keep_three, send_four, chosen = refs[:4]
    refs = refs[4:]
    bufs, (count, table_sem, small_sem, new_sem, kv_sem, weight_sem) = refs[:13], refs[13:]
    pairing, lengths, table, new_lengths, query, own, new_query, new_own, resid, new_resid, weight, new_buf, kv_buf = bufs
    new_cache, cache = ins[11], ins[12]
    z, x_lo = lax.axis_index("tp") // 2, lax.axis_index("tp") % 2
    width = weight.shape[1] // NZ

    table_copy = pltpu.make_async_copy(ins[2], table, table_sem)
    table_copy.start()
    small = [pltpu.make_async_copy(ins[n], bufs[n], small_sem.at[n]) for n in range(10) if n != 2]
    new_copy = pltpu.make_async_copy(new_cache, new_buf, new_sem)
    weight_copy = pltpu.make_async_copy(ins[10], weight, weight_sem)
    for copy in small:
        copy.start()
    new_copy.start()
    table_copy.wait()
    for e in range(4 * REQ):
        pltpu.make_async_copy(cache.at[table[e]], kv_buf.at[e], kv_sem).start()
    weight_copy.start()
    for copy in small:
        copy.wait()

    me = group_index()
    for j in range(REQ):
        count[j] = 0
    row = lax.broadcasted_iota(jnp.int32, (2 * REQ, REQ), 0)
    column = lax.broadcasted_iota(jnp.int32, (2 * REQ, REQ), 1)
    target_row = jnp.zeros((2 * REQ, REQ), jnp.int32)
    for i in range(REQ):
        target = pairing[i]
        k = count[target]
        count[target] = k + 1
        target_row = jnp.where(column == i, (me ^ target) * 2 + k, target_row)
    chosen[...] = jnp.where(row == target_row, 1.0, 0.0).astype(jnp.bfloat16)
    new_copy.wait()

    new_rows = attend(
        new_query[...],
        new_own[...],
        lambda r: new_buf[r],
        lambda r: new_lengths[r],
        new_buf.shape[1],
    )

    pltpu.make_async_copy(cache, kv_buf, kv_sem).wait()
    rows = attend(
        query[...],
        own[...],
        lambda r: kv_buf[4 * r : 4 * r + 4].reshape(4 * kv_buf.shape[1], 2 * HD),
        lambda r: lengths[r],
        4 * kv_buf.shape[1],
    )
    attended = jnp.concatenate([rows, new_rows], axis=0)
    weight_copy.wait()

    def part(flip):
        columns = pl.ds(pl.multiple_of((z ^ flip) * width, 128), width)
        return jnp.dot(attended, weight[:, columns], preferred_element_type=jnp.float32)

    for n, flip in enumerate((1, 3, 5, 7)):
        send_four[2 * REQ * n : 2 * REQ * (n + 1)] = part(flip).astype(jnp.bfloat16)
    for n, flip in enumerate((2, 4, 6)):
        keep_three[2 * REQ * n : 2 * REQ * (n + 1)] = part(flip)
    columns = pl.ds(pl.multiple_of(z * width, 128), width)
    block = jnp.concatenate([resid[:, columns], new_resid[:, columns]], axis=0)
    first[...] = part(0) + jnp.where(x_lo == 0, block.astype(jnp.float32), 0.0)


def front(*args):
    pairing, lengths, table, new_lengths, query, own, new_query, new_own, resid, new_resid, weight, new_cache, cache = args
    width = weight.shape[1] // NZ
    any_space = pl.BlockSpec(memory_space=pltpu.HBM)
    vmem = pl.BlockSpec(memory_space=VMEM)
    return pl.pallas_call(
        front_kernel,
        out_shape=[
            jax.ShapeDtypeStruct((2 * REQ, width), jnp.float32),
            jax.ShapeDtypeStruct((6 * REQ, width), jnp.float32),
            jax.ShapeDtypeStruct((8 * REQ, width), jnp.bfloat16),
            jax.ShapeDtypeStruct((2 * REQ, REQ), jnp.bfloat16),
        ],
        in_specs=[any_space] * 13,
        out_specs=[vmem] * 4,
        scratch_shapes=[SMEM(array.shape, array.dtype) for array in args[:4]]
        + [VMEM(array.shape, array.dtype) for array in args[4:12]]
        + [
            VMEM(cache.shape, jnp.bfloat16),
            SMEM((REQ,), jnp.int32),
            pltpu.SemaphoreType.DMA,
            pltpu.SemaphoreType.DMA((10,)),
            pltpu.SemaphoreType.DMA,
            pltpu.SemaphoreType.DMA,
            pltpu.SemaphoreType.DMA,
        ],
        compiler_params=pltpu.CompilerParams(vmem_limit_bytes=FRONT_LIMIT),
        cost_estimate=pl.CostEstimate(
            flops=400_000_000, bytes_accessed=9_500_000, transcendentals=30_000
        ),
        name="front",
    )(*args)


def spread_kernel(first, *refs):
    *parts, chosen, near, far = refs
    total = first[...]
    for part in parts:
        total = total + part[: 2 * REQ].astype(jnp.float32)
    half = total.astype(jnp.bfloat16)
    placed = jnp.dot(chosen[...], half[REQ:], preferred_element_type=jnp.float32)
    placed = placed.astype(jnp.bfloat16)
    near[:REQ] = half[:REQ]
    near[REQ:] = placed[:REQ]
    far[...] = placed[REQ:]


def finish_kernel(gain, *refs):
    *blocks, hidden, normed = refs
    z, me = lax.axis_index("tp") // 2, group_index()
    rows, width = hidden.shape[0], blocks[0].shape[1]
    slots = rows - REQ
    slot = lax.broadcasted_iota(jnp.int32, (slots, slots), 0)
    column = lax.broadcasted_iota(jnp.int32, (slots, slots), 1)
    offset = (slot >> 1) ^ me
    at = (offset & 1) * 16 + ((offset >> 1) & 3) * 4 + (offset >> 3) * 2 + (slot & 1)
    order = jnp.where(column == at, 1.0, 0.0).astype(jnp.bfloat16)
    square = jnp.zeros((rows, 1), jnp.float32)
    places = [(0, 0, 0), (0, 1, 2), (0, 2, 6), (0, 3, 4), (1, 0, 1), (1, 1, 3), (1, 2, 7), (1, 3, 5)]
    for n, part, shift in places:
        columns = pl.ds(pl.multiple_of((z ^ shift) * width, 128), width)
        block = blocks[n][rows * part : rows * (part + 1)]
        placed = jnp.dot(order, block[REQ:], preferred_element_type=jnp.float32)
        wide = jnp.concatenate([block[:REQ].astype(jnp.float32), placed], axis=0)
        hidden[:, columns] = wide.astype(jnp.bfloat16)
        square = square + jnp.sum(wide * wide, axis=-1, keepdims=True)
    inverse = lax.rsqrt(square / (width * NZ) + 1e-06)
    for k in range(NZ):
        columns = slice(k * width, (k + 1) * width)
        wide = hidden[:, columns].astype(jnp.float32)
        normed[:, columns] = (wide * inverse * gain[:, columns].astype(jnp.float32)).astype(
            jnp.bfloat16
        )


def place_kernel(pieces, part, *refs):
    whole, sem = refs[-2:]
    size = part.shape[0] // 4
    copies = []
    for n in range(4):
        for k in range(2):
            start, row, tokens = pieces[k]
            groups = pl.ds(n * size, size)
            source = part.at[groups, pl.ds(row, tokens)]
            target = whole.at[groups, k, pl.ds(start, tokens)]
            copies.append(pltpu.make_async_copy(source, target, sem.at[2 * n + k]))
    for copy in copies:
        copy.start()
    for copy in copies:
        copy.wait()


def place(part, late, whole):
    given = [part] if isinstance(whole, tuple) else [part, whole]
    shape = whole if isinstance(whole, tuple) else whole.shape
    hbm = pl.BlockSpec(memory_space=pltpu.HBM)
    return pl.pallas_call(
        functools.partial(place_kernel, pieces_of(late, shape[2])),
        out_shape=jax.ShapeDtypeStruct(shape, part.dtype),
        in_specs=[pl.BlockSpec(memory_space=VMEM)] + [hbm] * (len(given) - 1),
        out_specs=hbm,
        scratch_shapes=[pltpu.SemaphoreType.DMA((8,))],
        compiler_params=pltpu.CompilerParams(vmem_limit_bytes=SMALL_LIMIT),
        input_output_aliases={} if len(given) == 1 else {1: 0},
        cost_estimate=pl.CostEstimate(flops=0, bytes_accessed=2 * part.size * 2, transcendentals=0),
        name="place",
    )(*given)


def body(
    cache,
    table,
    lengths,
    query,
    step_kv,
    resid,
    new_cache,
    new_lengths,
    new_query,
    new_step_kv,
    new_resid,
    pairing,
    o_weight,
    norm_gain,
):
    pools, groups = lax.axis_size("pool"), lax.axis_size("pool") * lax.axis_size("group")
    ranks = lax.axis_size("tp")
    pair = pairing[0, 0, :, 0]
    prompts = new_cache[0, 0, :, :, 0]
    vmem = pl.BlockSpec(memory_space=VMEM)
    both = ("pool", "group")

    def over_tp(array, flip):
        return lax.ppermute(array, "tp", [(t, t ^ flip) for t in range(ranks)])

    def over_groups(array, flip):
        return lax.ppermute(array, both, [(s, s ^ flip) for s in range(groups)])

    def deliver(array):
        return lax.all_to_all(array, both, split_axis=0, concat_axis=0, tiled=True)

    prompt = (pair, new_lengths[0, 0], new_step_kv[0, 0, :, 0], prompts)
    early = deliver(pack(*prompt, False))
    late = pack(*prompt, True)

    first, keep_three, send_four, chosen = front(
        pair,
        lengths[0, 0],
        table[0, 0],
        new_lengths[0, 0],
        query[0, 0],
        step_kv[0, 0, :, 0],
        new_query[0, 0],
        new_step_kv[0, 0, :, 0],
        resid[0, 0],
        new_resid[0, 0],
        o_weight,
        prompts,
        cache[0, 0, :, :, 0],
    )
    four, gain, late = lax.optimization_barrier(
        (over_tp(send_four, 2), norm_gain.reshape(1, -1), late)
    )
    parts = [four]
    for n, flip in ((0, 2), (2, 6), (1, 4)):
        summed = keep_three[2 * REQ * n : 2 * REQ * (n + 1)]
        summed = summed + four[2 * REQ * (n + 1) : 2 * REQ * (n + 2)].astype(jnp.float32)
        parts.append(over_tp(summed.astype(jnp.bfloat16), 2 * flip))
    width = first.shape[1]
    near, far = pl.pallas_call(
        spread_kernel,
        out_shape=[
            jax.ShapeDtypeStruct((2 * REQ, width), jnp.bfloat16),
            jax.ShapeDtypeStruct((REQ, width), jnp.bfloat16),
        ],
        in_specs=[vmem] * (len(parts) + 2),
        out_specs=[vmem] * 2,
        compiler_params=pltpu.CompilerParams(vmem_limit_bytes=SMALL_LIMIT),
        name="spread",
    )(first, *parts, chosen)

    across = [(n, n ^ (ranks + 1)) for n in range(pools * ranks)]
    far_here = over_groups(far, groups // 2)
    far_there = lax.ppermute(far, ("pool", "tp"), across)
    near_there = over_tp(near, 1)
    near = (near.astype(jnp.float32) + near_there.astype(jnp.float32)).astype(jnp.bfloat16)
    far = (far_here.astype(jnp.float32) + far_there.astype(jnp.float32)).astype(jnp.bfloat16)
    toward = [
        jnp.concatenate([near[REQ + 4 * y : REQ + 4 * y + 4], far[4 * y : 4 * y + 4]], axis=0)
        for y in range(4)
    ]
    slots = [toward[0]] + [over_groups(toward[y], 2 * y) for y in range(1, 4)]
    late, *slots = lax.optimization_barrier((late, *slots))
    late = deliver(late)
    slots = jnp.stack(slots).reshape(4, 2, 2, 2, width)
    kept, given = (slots[:, :, c].reshape(REQ, width) for c in range(2))
    block = jnp.concatenate([near[:REQ], kept, over_groups(given, 1)], axis=0)

    slot_cache = place(early, False, (groups, 2) + prompts.shape[1:])
    flips = [over_tp(block, 2 * k) for k in (2, 6, 4)]
    *flips, slot_cache = lax.optimization_barrier((*flips, slot_cache))
    four = jnp.concatenate([block, *flips], axis=0)
    blocks = [four, over_tp(four, 2)]
    hidden, normed = pl.pallas_call(
        finish_kernel,
        out_shape=[jax.ShapeDtypeStruct((block.shape[0], width * NZ), jnp.bfloat16)] * 2,
        in_specs=[vmem] * (len(blocks) + 1),
        out_specs=[vmem] * 2,
        compiler_params=pltpu.CompilerParams(vmem_limit_bytes=SMALL_LIMIT),
        cost_estimate=pl.CostEstimate(flops=0, bytes_accessed=4_000_000, transcendentals=0),
        name="finish",
    )(gain, *blocks)

    late, hidden = lax.optimization_barrier((late, hidden))
    slot_cache = place(late, True, slot_cache).reshape((2 * groups,) + prompts.shape[1:])
    return (hidden[None, None], normed[None, None], slot_cache[None, None, :, :, None, :])


def solution(mesh):
    placed = (
        P("pool", "group", None, None, "tp", None),
        P("pool", "group", None),
        P("pool", "group", None),
        P("pool", "group", None, "tp"),
        P("pool", "group", None, "tp", None),
        P("pool", "group", None, None),
        P("pool", "group", None, None, "tp", None),
        P("pool", "group", None),
        P("pool", "group", None, "tp"),
        P("pool", "group", None, "tp", None),
        P("pool", "group", None, None),
        P("pool", "group", None, None),
        P("tp", None),
        P(),
    )
    return jax.shard_map(
        body,
        mesh=mesh,
        in_specs=placed,
        out_specs=(
            P("pool", "group", None, None),
            P("pool", "group", None, None),
            P("pool", "group", None, None, "tp", None),
        ),
        check_vma=False,
    )
```
